32 devices in a mesh: ctx: 8 (over y, x, core), mp: 4 (over z).
Axes of the slice: x: 2, y: 2, z: 4, core: 2. Of those that a mesh axis runs over, the one named last changes fastest.
Arguments:
- queries: bfloat16 [2048, 8192], P('ctx', 'mp'), may hold values from -6 to 6
- key_feats: bfloat16 [2048, 8192], P('ctx', 'mp'), may hold values from -6 to 6
- value_feats: bfloat16 [2048, 8192], P('ctx', 'mp'), may hold values from -6 to 6
- filters: bfloat16 [512, 128], P('mp'), may hold values from -0.5 to 0.5
- grad_out: bfloat16 [2048, 8192], P('ctx', 'mp'), may hold values from -40 to 40
Outputs:
- mixer_out: bfloat16 [2048, 8192], P('ctx', 'mp')
- grad_queries: bfloat16 [2048, 8192], P('ctx', 'mp')
- grad_keys: bfloat16 [2048, 8192], P('ctx', 'mp')
- grad_values: bfloat16 [2048, 8192], P('ctx', 'mp')
- grad_filters: float32 [512, 128], P('mp')
The draws below stay inside these ranges and needn't reach their ends.
All inputs are finite; a program needn't handle non-finite values.
Results may differ from the reference program's by a relative error of at most 0.0058.
Values may be sent and summed in bfloat16 or wider, within the bound.
A program may use at most 64 MiB of HBM per device.

```python
import jax
import jax.numpy as jnp
from jax import lax

D = 8192
G = 16
K = 128
LENGTH = 2048
GROUPS = 512


def draw_grad_out(key, part):
    first_key = jax.random.fold_in(key, 11)
    second_key = jax.random.fold_in(key, 23)
    position = jnp.arange(D, dtype=jnp.float32) / D
    token_scale = jnp.exp(jax.random.uniform(second_key, (LENGTH, 1), minval=-0.7, maxval=0.7))
    basic = jnp.clip(jax.random.normal(first_key, (LENGTH, D)), -6.0, 6.0)
    channel_scale = 10.0 ** (position - 0.5)
    return (basic * token_scale * channel_scale[None, :]).astype(jnp.bfloat16)


def level_of(key, dims, cuts, smallest, high):
    factor_of, own = 1.0, jax.random.fold_in(key, 6)
    for axis_at, parts in cuts:
        heights = jnp.exp(jax.random.uniform(jax.random.fold_in(own, axis_at), (parts,), jnp.float32, smallest / len(cuts), high / len(cuts)))
        factor_of = factor_of * jnp.repeat(heights, dims[axis_at] // parts).reshape([-1 if axis == axis_at else 1 for axis in range(len(dims))])
    return factor_of


def gaussian(stream_key, extent, scale, bound, cuts=(), kind=jnp.bfloat16):
    values = scale * jax.random.normal(stream_key, extent, jnp.float32)
    if cuts:
        values = values * level_of(stream_key, extent, cuts, -0.22, 0.18)
    return jnp.clip(values, -bound, bound).astype(kind)


def setup_inputs(seed: int = 0) -> dict:
    splits = jax.random.split(jax.random.key(seed), 6)
    return {
        "queries": gaussian(splits[0], (LENGTH, D), 1.0, 6.0, ((0, 8), (1, 4))),
        "key_feats": gaussian(splits[1], (LENGTH, D), 1.0, 6.0, ((0, 8), (1, 4))),
        "value_feats": gaussian(splits[2], (LENGTH, D), 1.0, 6.0, ((0, 8), (1, 4))),
        "filters": gaussian(splits[3], (GROUPS, K), K ** -0.5, 0.5, ((0, 4),)),
        "grad_out": draw_grad_out(jax.random.fold_in(splits[5], 71), 0),
    }


def contract(formula, first_op, second_op):
    return jnp.einsum(formula, first_op.astype(jnp.float32), second_op.astype(jnp.float32), precision=lax.Precision.HIGHEST)

def toeplitz(filt):
    count, filter_len = filt.shape
    flipped = filt[:, ::-1]
    lead_zero = jnp.zeros((count, 1), filt.dtype)
    trailing = jnp.zeros((count, filter_len), filt.dtype)
    pattern = jnp.concatenate([lead_zero, flipped, trailing], axis=1)
    repeated = jnp.tile(pattern, (1, filter_len))
    return repeated[:, :filter_len * 2 * filter_len].reshape(count, filter_len, 2 * filter_len)

def make_windows(blocks, before):
    earlier = jnp.concatenate([before[:, :, None, :], blocks[:, :, :-1, :]], axis=2)
    return jnp.concatenate([earlier, blocks], axis=3)

def forward_conv(signal, before, toeplitz_mat):
    groups_here, group_size, seq_len = signal.shape
    filter_len = toeplitz_mat.shape[1]
    blocks = signal.reshape(groups_here, group_size, seq_len // filter_len, filter_len)
    window_rows = make_windows(blocks, before)
    result = contract('gam,gsnm->gsna', toeplitz_mat, window_rows)
    return (result.reshape(groups_here, group_size, seq_len), window_rows)

def backward_conv(grad_rows, after, toeplitz_mat):
    groups_here, group_size, seq_len = grad_rows.shape
    filter_len = toeplitz_mat.shape[1]
    blocks = grad_rows.reshape(groups_here, group_size, seq_len // filter_len, filter_len)
    spread = contract('gam,gsna->gsnm', toeplitz_mat, blocks)
    tail_part = contract('gam,gsa->gsm', toeplitz_mat, after)
    next_part = jnp.concatenate([spread[:, :, 1:, :filter_len], tail_part[:, :, None, :filter_len]], axis=2)
    return (spread[:, :, :, filter_len:] + next_part).reshape(groups_here, group_size, seq_len)

def filter_grad(grad_rows, window_rows, filter_len):
    groups_here, group_size, seq_len = grad_rows.shape
    blocks = grad_rows.reshape(groups_here, group_size, seq_len // filter_len, filter_len)
    correlate = contract('gsna,gsnm->gam', blocks, window_rows)
    flattened = correlate.reshape(groups_here, filter_len * 2 * filter_len)
    flattened = jnp.concatenate([flattened, jnp.zeros((groups_here, filter_len), jnp.float32)], axis=1)
    flattened = flattened.reshape(groups_here, filter_len, 2 * filter_len + 1)
    diagonals = lax.optimization_barrier(jnp.sum(flattened, axis=1))
    return diagonals[:, 1:filter_len + 1][:, ::-1]

def reference(queries, key_feats, value_feats, filters, grad_out):
    seq_len, channels = queries.shape
    slab_width = 1024
    slab_groups = slab_width // G
    outs_mixer, outs_query, outs_key, outs_value, outs_filter = ([], [], [], [], [])
    for slab_index in range(channels // slab_width):
        lower = slab_index * slab_width
        query_f = queries[:, lower:lower + slab_width].astype(jnp.float32)
        key_f = key_feats[:, lower:lower + slab_width].astype(jnp.float32)
        value_f = value_feats[:, lower:lower + slab_width].astype(jnp.float32)
        cot_f = grad_out[:, lower:lower + slab_width].astype(jnp.float32)
        own_filters = filters[slab_index * slab_groups:(slab_index + 1) * slab_groups]
        product = (key_f * value_f).astype(jnp.bfloat16)
        grad_mix = (cot_f * query_f).astype(jnp.bfloat16)
        signal = product.T.reshape(slab_groups, G, seq_len)
        grad_rows = grad_mix.T.reshape(slab_groups, G, seq_len)
        zero_rim = jnp.zeros((slab_groups, G, K), jnp.bfloat16)
        toeplitz_mat = toeplitz(own_filters)
        conv_out, window_rows = forward_conv(signal, zero_rim, toeplitz_mat)
        conv_out = conv_out.astype(jnp.bfloat16)
        conv_grad = backward_conv(grad_rows, zero_rim, toeplitz_mat).astype(jnp.bfloat16)
        outs_filter.append(filter_grad(grad_rows, window_rows, K))
        conv_f = conv_out.reshape(slab_width, seq_len).T.astype(jnp.float32)
        back_f = conv_grad.reshape(slab_width, seq_len).T.astype(jnp.float32)
        outs_mixer.append((query_f * conv_f).astype(jnp.bfloat16))
        outs_query.append((cot_f * conv_f).astype(jnp.bfloat16))
        outs_key.append((back_f * value_f).astype(jnp.bfloat16))
        outs_value.append((back_f * key_f).astype(jnp.bfloat16))
    raw_filters = jnp.concatenate(outs_filter, axis=0)
    grad_rms = jnp.sqrt(jnp.mean(raw_filters * raw_filters) + 1e-06)
    grad_filters = raw_filters * jnp.minimum(1.0, 1.0 / grad_rms)
    return (jnp.concatenate(outs_mixer, axis=1), jnp.concatenate(outs_query, axis=1), jnp.concatenate(outs_key, axis=1), jnp.concatenate(outs_value, axis=1), grad_filters)
```

```python
import functools

import jax
import jax.numpy as jnp
from jax import lax
from jax.experimental import pallas as pl
from jax.experimental.pallas import tpu as pltpu
from jax.sharding import PartitionSpec as P

G = 16
MESH = pl.DeviceIdType.MESH
F32 = jnp.float32
BF16 = jnp.bfloat16
WIDE = 128
PARTS = 4


def times(a, b):
    return (a.astype(F32) * b.astype(F32)).astype(BF16)


def rows_dot(a, b):
    return lax.dot_general(a, b, (((1,), (1,)), ((), ())), preferred_element_type=F32)


def kernel(n_ctx, n_mp, q_ref, k_ref, v_ref, f_ref, g_ref,
           mix_ref, gq_ref, gk_ref, gv_ref, gf_ref,
           prod, gmix, phalo, ghalo, taps, toep, pt, gt, folded,
           partial, arrived, reduced, gathered, own_sq, all_sq,
           p_send, p_recv, g_send, g_recv,
           rs_send, rs_recv, ag_send, ag_recv, sq_send, sq_recv):
    tokens, channels = q_ref.shape
    groups, span = f_ref.shape
    blocks = tokens // span
    own = groups // n_ctx
    part = channels // PARTS
    me = lax.axis_index("ctx")
    slab = lax.axis_index("mp")
    per_chunk = WIDE // G

    def ctx_peer(i):
        return lax.rem(me + i, n_ctx)

    def mp_peer(i):
        return lax.rem(slab + i, n_mp)

    barrier = pltpu.get_barrier_semaphore()

    @pl.loop(1, n_ctx)
    def _(i):
        pl.semaphore_signal(barrier, inc=1, device_id=(ctx_peer(i), slab), device_id_type=MESH)

    @pl.loop(1, n_mp)
    def _(i):
        pl.semaphore_signal(barrier, inc=1, device_id=(me, mp_peer(i)), device_id_type=MESH)

    head, tail = slice(0, span), slice(tokens - span, tokens)
    gmix[head, :] = times(g_ref[head, :], q_ref[head, :])
    prod[tail, :] = times(k_ref[tail, :], v_ref[tail, :])
    pl.semaphore_wait(barrier, n_ctx + n_mp - 2)

    def g_copy(i):
        cols = slice(i * part, (i + 1) * part)
        return pltpu.make_async_remote_copy(
            src_ref=gmix.at[head, cols], dst_ref=ghalo.at[:, cols],
            send_sem=g_send.at[i], recv_sem=g_recv.at[i],
            device_id=(lax.rem(me + n_ctx - 1, n_ctx), slab), device_id_type=MESH)

    def p_copy(i):
        cols = slice(i * part, (i + 1) * part)
        return pltpu.make_async_remote_copy(
            src_ref=prod.at[tail, cols], dst_ref=phalo.at[:, cols],
            send_sem=p_send.at[i], recv_sem=p_recv.at[i],
            device_id=(lax.rem(me + 1, n_ctx), slab), device_id_type=MESH)

    for i in range(PARTS):
        @pl.when(me > 0)
        def _():
            g_copy(i).start()

        @pl.when(me < n_ctx - 1)
        def _():
            p_copy(i).start()

    @pl.when(me == 0)
    def _():
        phalo[...] = jnp.zeros_like(phalo)

    @pl.when(me == n_ctx - 1)
    def _():
        ghalo[...] = jnp.zeros_like(ghalo)

    rest_g, rest_p = slice(span, tokens), slice(0, tokens - span)
    gmix[rest_g, :] = times(g_ref[rest_g, :], q_ref[rest_g, :])
    prod[rest_p, :] = times(k_ref[rest_p, :], v_ref[rest_p, :])
    taps[...] = f_ref[...].astype(F32)

    col = lax.broadcasted_iota(jnp.int32, (span, span), 1)
    row = lax.broadcasted_iota(jnp.int32, (span, span), 0)
    upper = col >= row

    @pl.loop(0, groups)
    def _(i):
        line = jnp.broadcast_to(taps[pl.ds(i, 1), :], (span, span))
        turned = pltpu.roll(line, 0, 1, stride=1, stride_axis=0)
        zero = jnp.zeros_like(turned)
        toep[i, :, 0:span] = jnp.where(upper, turned, zero).astype(BF16)
        toep[i, :, span:] = jnp.where(upper, zero, turned).astype(BF16)

    @pl.loop(0, channels // WIDE)
    def _(c):
        at = pl.ds(pl.multiple_of(c * WIDE, WIDE), WIDE)
        pt[at, span:] = prod[:, at].T
        gt[at, 0:tokens] = gmix[:, at].T

    @pl.when(me < n_ctx - 1)
    def _():
        for i in range(PARTS):
            g_copy(i).wait_recv()

    @pl.loop(0, channels // WIDE)
    def _(c):
        at = pl.ds(pl.multiple_of(c * WIDE, WIDE), WIDE)
        gt[at, tokens:] = ghalo[:, at].T

    def windows(ref, at):
        x = ref[at, :]
        return jnp.concatenate(
            [x[:, n * span:(n + 2) * span] for n in range(blocks)], axis=0)

    @pl.loop(0, groups)
    def _(i):
        at = pl.ds(pl.multiple_of(i * G, G), G)
        x = pt[at, :]
        left = jnp.concatenate(
            [x[:, (n + 1) * span:(n + 2) * span] for n in range(blocks)], axis=0)
        both = lax.dot_general(left, windows(gt, at), (((0,), (0,)), ((), ())),
                               preferred_element_type=F32)
        turn = jnp.where(upper, both[:, :span], both[:, span:])
        half = span // 2
        while half >= 8:
            turn = turn[:half] + pltpu.roll(turn[half:], span - half, 1)
            half //= 2
        folded[pl.ds(pl.multiple_of(i * 8, 8), 8), :] = turn

    total = folded[pl.ds(0, groups, stride=8), :]
    for r in range(1, 8):
        total = total + pltpu.roll(folded[pl.ds(r, groups, stride=8), :], span - r, 1)
    partial[...] = total.reshape(partial.shape)

    def rs_copy(to, sender):
        return pltpu.make_async_remote_copy(
            src_ref=partial.at[to], dst_ref=arrived.at[sender],
            send_sem=rs_send.at[to], recv_sem=rs_recv.at[sender],
            device_id=(to, slab), device_id_type=MESH)

    def ag_copy(to, sender):
        return pltpu.make_async_remote_copy(
            src_ref=reduced, dst_ref=gathered.at[sender],
            send_sem=ag_send.at[to], recv_sem=ag_recv.at[sender],
            device_id=(to, slab), device_id_type=MESH)

    def sq_copy(to, sender):
        return pltpu.make_async_remote_copy(
            src_ref=own_sq, dst_ref=all_sq.at[sender],
            send_sem=sq_send.at[to], recv_sem=sq_recv.at[sender],
            device_id=(me, to), device_id_type=MESH)

    @pl.loop(1, n_ctx)
    def _(i):
        rs_copy(ctx_peer(i), me).start()

    arrived[me] = partial[me]

    @pl.loop(0, channels // WIDE)
    def _(c):
        at = pl.ds(pl.multiple_of(c * WIDE, WIDE), WIDE)
        rows = []
        for j in range(per_chunk):
            mine = pl.ds(pl.multiple_of(c * WIDE + j * G, G), G)
            y = rows_dot(windows(gt, mine), toep[c * per_chunk + j])
            rows.append(jnp.concatenate(
                [y[n * G:(n + 1) * G] for n in range(blocks)], axis=1))
        back = jnp.concatenate(rows, axis=0).astype(BF16).T
        gk_ref[:, at] = times(back, v_ref[:, at])
        gv_ref[:, at] = times(back, k_ref[:, at])

    @pl.loop(1, n_ctx)
    def _(i):
        rs_copy(me, ctx_peer(i)).wait_recv()

    reduced[...] = jnp.sum(arrived[...], axis=0)

    @pl.loop(1, n_ctx)
    def _(i):
        ag_copy(ctx_peer(i), me).start()

    gathered[me] = reduced[...]

    @pl.when(me > 0)
    def _():
        for i in range(PARTS):
            p_copy(i).wait_recv()

    @pl.loop(0, channels // WIDE)
    def _(c):
        at = pl.ds(pl.multiple_of(c * WIDE, WIDE), WIDE)
        pt[at, 0:span] = phalo[:, at].T
        rows = []
        for j in range(per_chunk):
            mine = pl.ds(pl.multiple_of(c * WIDE + j * G, G), G)
            u = toep[c * per_chunk + j]
            turned = jnp.concatenate([u[:, span:], u[:, :span]], axis=0)
            y = jnp.dot(windows(pt, mine), turned, preferred_element_type=F32)
            rows.append(jnp.concatenate(
                [y[n * G:(n + 1) * G] for n in range(blocks)], axis=1))
        conv = jnp.concatenate(rows, axis=0).astype(BF16).T
        mix_ref[:, at] = times(conv, q_ref[:, at])
        gq_ref[:, at] = times(conv, g_ref[:, at])

    @pl.loop(1, n_ctx)
    def _(i):
        ag_copy(me, ctx_peer(i)).wait_recv()

    raw = gathered[...].reshape(groups, span)
    squares = jnp.sum(jnp.sum(raw * raw, axis=0, keepdims=True), axis=1, keepdims=True)
    own_sq[...] = jnp.broadcast_to(squares, own_sq.shape)

    @pl.loop(1, n_mp)
    def _(i):
        sq_copy(mp_peer(i), slab).start()

    all_sq[slab] = own_sq[...]

    @pl.loop(1, n_mp)
    def _(i):
        sq_copy(slab, mp_peer(i)).wait_recv()

    square_sum = jnp.sum(all_sq[...], axis=0)[0:1, :]
    grad_rms = jnp.sqrt(square_sum / (groups * n_mp * span) + 1e-06)
    gf_ref[...] = raw * jnp.minimum(1.0, 1.0 / grad_rms)

    for i in range(PARTS):
        @pl.when(me > 0)
        def _():
            g_copy(i).wait_send()

        @pl.when(me < n_ctx - 1)
        def _():
            p_copy(i).wait_send()

    @pl.loop(1, n_ctx)
    def _(i):
        rs_copy(ctx_peer(i), me).wait_send()
        ag_copy(ctx_peer(i), me).wait_send()

    @pl.loop(1, n_mp)
    def _(i):
        sq_copy(mp_peer(i), slab).wait_send()


def shards(queries, key_feats, value_feats, filters, grad_out):
    n_ctx, n_mp = lax.axis_size("ctx"), lax.axis_size("mp")
    tokens, channels = queries.shape
    groups, span = filters.shape
    own = groups // n_ctx
    vmem = pl.BlockSpec(memory_space=pltpu.VMEM)
    dma = pltpu.SemaphoreType.DMA
    like = jax.ShapeDtypeStruct((tokens, channels), BF16)
    return pl.pallas_call(
        functools.partial(kernel, n_ctx, n_mp),
        out_shape=(like, like, like, like, jax.ShapeDtypeStruct((groups, span), F32)),
        in_specs=[vmem] * 5,
        out_specs=[vmem] * 5,
        scratch_shapes=[
            pltpu.VMEM((tokens, channels), BF16),
            pltpu.VMEM((tokens, channels), BF16),
            pltpu.VMEM((span, channels), BF16),
            pltpu.VMEM((span, channels), BF16),
            pltpu.VMEM((groups, span), F32),
            pltpu.VMEM((groups, span, 2 * span), BF16),
            pltpu.VMEM((channels, tokens + span), BF16),
            pltpu.VMEM((channels, tokens + span), BF16),
            pltpu.VMEM((8 * groups, span), F32),
            pltpu.VMEM((n_ctx, own, span), F32),
            pltpu.VMEM((n_ctx, own, span), F32),
            pltpu.VMEM((own, span), F32),
            pltpu.VMEM((n_ctx, own, span), F32),
            pltpu.VMEM((8, span), F32),
            pltpu.VMEM((n_mp, 8, span), F32),
            dma((PARTS,)), dma((PARTS,)), dma((PARTS,)), dma((PARTS,)),
            dma((n_ctx,)), dma((n_ctx,)), dma((n_ctx,)), dma((n_ctx,)),
            dma((n_mp,)), dma((n_mp,)),
        ],
        compiler_params=pltpu.CompilerParams(
            collective_id=0, has_side_effects=True, vmem_limit_bytes=56 * 2**20),
    )(queries, key_feats, value_feats, filters, grad_out)


def solution(mesh):
    placed = (P("ctx", "mp"), P("ctx", "mp"), P("ctx", "mp"), P("mp", None), P("ctx", "mp"))
    return jax.shard_map(
        shards,
        mesh=mesh,
        in_specs=placed,
        out_specs=(P("ctx", "mp"), P("ctx", "mp"), P("ctx", "mp"), P("ctx", "mp"), P("mp", None)),
        check_vma=False,
    )
```

```python
import functools

import jax
import jax.numpy as jnp
from jax import lax
from jax.experimental import pallas as pl
from jax.experimental.pallas import tpu as pltpu
from jax.sharding import PartitionSpec as P

G = 16
MESH = pl.DeviceIdType.MESH
F32 = jnp.float32
BF16 = jnp.bfloat16
WIDE = 128
PARTS = 4


def times(a, b):
    return (a.astype(F32) * b.astype(F32)).astype(BF16)


def kernel(n_ctx, n_mp, q_ref, k_ref, v_ref, f_ref, g_ref,
           mix_ref, gq_ref, gk_ref, gv_ref, gf_ref,
           prod, gmix, phalo, ghalo, taps, flipped, toep, toep_f, folded,
           partial, arrived, reduced, gathered, own_sq, all_sq,
           p_send, p_recv, g_send, g_recv,
           rs_send, rs_recv, ag_send, ag_recv, sq_send, sq_recv):
    tokens, channels = q_ref.shape
    groups, span = f_ref.shape
    blocks = tokens // span
    own = groups // n_ctx
    part = channels // PARTS
    me = lax.axis_index("ctx")
    slab = lax.axis_index("mp")
    per_chunk = WIDE // G

    def ctx_peer(i):
        return lax.rem(me + i, n_ctx)

    def mp_peer(i):
        return lax.rem(slab + i, n_mp)

    barrier = pltpu.get_barrier_semaphore()

    @pl.loop(1, n_ctx)
    def _(i):
        pl.semaphore_signal(barrier, inc=1, device_id=(ctx_peer(i), slab), device_id_type=MESH)

    @pl.loop(1, n_mp)
    def _(i):
        pl.semaphore_signal(barrier, inc=1, device_id=(me, mp_peer(i)), device_id_type=MESH)

    head, tail = slice(0, span), slice(tokens - span, tokens)
    gmix[head, :] = times(g_ref[head, :], q_ref[head, :])
    prod[tail, :] = times(k_ref[tail, :], v_ref[tail, :])
    pl.semaphore_wait(barrier, n_ctx + n_mp - 2)

    def g_copy(i):
        cols = slice(i * part, (i + 1) * part)
        return pltpu.make_async_remote_copy(
            src_ref=gmix.at[head, cols], dst_ref=ghalo.at[:, cols],
            send_sem=g_send.at[i], recv_sem=g_recv.at[i],
            device_id=(lax.rem(me + n_ctx - 1, n_ctx), slab), device_id_type=MESH)

    def p_copy(i):
        cols = slice(i * part, (i + 1) * part)
        return pltpu.make_async_remote_copy(
            src_ref=prod.at[tail, cols], dst_ref=phalo.at[:, cols],
            send_sem=p_send.at[i], recv_sem=p_recv.at[i],
            device_id=(lax.rem(me + 1, n_ctx), slab), device_id_type=MESH)

    for i in range(PARTS):
        @pl.when(me > 0)
        def _():
            g_copy(i).start()

        @pl.when(me < n_ctx - 1)
        def _():
            p_copy(i).start()

    @pl.when(me == 0)
    def _():
        phalo[...] = jnp.zeros_like(phalo)

    @pl.when(me == n_ctx - 1)
    def _():
        ghalo[...] = jnp.zeros_like(ghalo)

    rest_g, rest_p = slice(span, tokens), slice(0, tokens - span)
    gmix[rest_g, :] = times(g_ref[rest_g, :], q_ref[rest_g, :])
    prod[rest_p, :] = times(k_ref[rest_p, :], v_ref[rest_p, :])
    taps[...] = f_ref[...].astype(F32)

    col = lax.broadcasted_iota(jnp.int32, (span, span), 1)
    row = lax.broadcasted_iota(jnp.int32, (span, span), 0)
    upper = col >= row

    flip = jnp.where(lax.rem(row + col, span) == 0, 1.0, 0.0).astype(BF16)
    flipped[...] = jnp.dot(f_ref[...], flip, preferred_element_type=F32)

    def spread(i, lines, out, mask):
        line = jnp.broadcast_to(lines[pl.ds(i, 1), :], (span, span))
        turned = pltpu.roll(line, 0, 1, stride=1, stride_axis=0)
        zero = jnp.zeros_like(turned)
        out[i, :, 0:span] = jnp.where(mask, turned, zero).astype(BF16)
        out[i, :, span:] = jnp.where(mask, zero, turned).astype(BF16)

    @pl.loop(0, groups // per_chunk)
    def _(c):
        for j in range(per_chunk):
            spread(c * per_chunk + j, taps, toep, upper)
            spread(c * per_chunk + j, flipped, toep_f, col > row)

    lane = lax.broadcasted_iota(jnp.int32, (1, blocks * WIDE), 1)
    member = lax.rem(lane, WIDE) // G

    def g_windows(at):
        own_part = gmix[:, at]
        last = jnp.concatenate([gmix[tail, at], ghalo[:, at]], axis=0)
        wins = [own_part[n * span:(n + 2) * span] for n in range(blocks - 1)]
        return jnp.concatenate(wins + [last], axis=1)

    def p_windows(at):
        own_part = prod[:, at]
        first = jnp.concatenate([phalo[:, at], prod[head, at]], axis=0)
        wins = [own_part[(n - 1) * span:(n + 1) * span] for n in range(1, blocks)]
        return jnp.concatenate([first] + wins, axis=1)

    def conv(c, mats, wins):
        out = None
        for j in range(per_chunk):
            y = jnp.dot(mats[c * per_chunk + j], wins, preferred_element_type=F32)
            out = y if out is None else jnp.where(member == j, y, out)
        out = out.astype(BF16)
        return jnp.concatenate(
            [out[:, n * WIDE:(n + 1) * WIDE] for n in range(blocks)], axis=0)

    @pl.when(me < n_ctx - 1)
    def _():
        for i in range(PARTS):
            g_copy(i).wait_recv()

    @pl.loop(0, channels // WIDE)
    def _(c):
        at = pl.ds(pl.multiple_of(c * WIDE, WIDE), WIDE)
        wins = g_windows(at).T
        left = jnp.concatenate(
            [prod[n * span:(n + 1) * span, at] for n in range(blocks)], axis=1)
        for j in range(per_chunk):
            mine = jnp.where(member == j, left, jnp.zeros_like(left))
            both = jnp.dot(mine, wins, preferred_element_type=F32)
            turn = jnp.where(upper, both[:, :span], both[:, span:])
            half = span // 2
            while half >= 8:
                turn = turn[:half] + pltpu.roll(turn[half:], span - half, 1)
                half //= 2
            folded[pl.ds(pl.multiple_of((c * per_chunk + j) * 8, 8), 8), :] = turn

    total = folded[pl.ds(0, groups, stride=8), :]
    for r in range(1, 8):
        total = total + pltpu.roll(folded[pl.ds(r, groups, stride=8), :], span - r, 1)
    partial[...] = total.reshape(partial.shape)

    def rs_copy(to, sender):
        return pltpu.make_async_remote_copy(
            src_ref=partial.at[to], dst_ref=arrived.at[sender],
            send_sem=rs_send.at[to], recv_sem=rs_recv.at[sender],
            device_id=(to, slab), device_id_type=MESH)

    def ag_copy(to, sender):
        return pltpu.make_async_remote_copy(
            src_ref=reduced, dst_ref=gathered.at[sender],
            send_sem=ag_send.at[to], recv_sem=ag_recv.at[sender],
            device_id=(to, slab), device_id_type=MESH)

    def sq_copy(to, sender):
        return pltpu.make_async_remote_copy(
            src_ref=own_sq, dst_ref=all_sq.at[sender],
            send_sem=sq_send.at[to], recv_sem=sq_recv.at[sender],
            device_id=(me, to), device_id_type=MESH)

    @pl.loop(1, n_ctx)
    def _(i):
        rs_copy(ctx_peer(i), me).start()

    arrived[me] = partial[me]

    @pl.loop(0, channels // WIDE)
    def _(c):
        at = pl.ds(pl.multiple_of(c * WIDE, WIDE), WIDE)
        back = conv(c, toep, g_windows(at))
        gk_ref[:, at] = times(back, v_ref[:, at])
        gv_ref[:, at] = times(back, k_ref[:, at])

    @pl.loop(1, n_ctx)
    def _(i):
        rs_copy(me, ctx_peer(i)).wait_recv()

    reduced[...] = jnp.sum(arrived[...], axis=0)

    @pl.loop(1, n_ctx)
    def _(i):
        ag_copy(ctx_peer(i), me).start()

    gathered[me] = reduced[...]

    @pl.when(me > 0)
    def _():
        for i in range(PARTS):
            p_copy(i).wait_recv()

    @pl.loop(0, channels // WIDE)
    def _(c):
        at = pl.ds(pl.multiple_of(c * WIDE, WIDE), WIDE)
        ahead = conv(c, toep_f, p_windows(at))
        mix_ref[:, at] = times(ahead, q_ref[:, at])
        gq_ref[:, at] = times(ahead, g_ref[:, at])

    @pl.loop(1, n_ctx)
    def _(i):
        ag_copy(me, ctx_peer(i)).wait_recv()

    raw = gathered[...].reshape(groups, span)
    squares = jnp.sum(jnp.sum(raw * raw, axis=0, keepdims=True), axis=1, keepdims=True)
    own_sq[...] = jnp.broadcast_to(squares, own_sq.shape)

    @pl.loop(1, n_mp)
    def _(i):
        sq_copy(mp_peer(i), slab).start()

    all_sq[slab] = own_sq[...]

    @pl.loop(1, n_mp)
    def _(i):
        sq_copy(slab, mp_peer(i)).wait_recv()

    square_sum = jnp.sum(all_sq[...], axis=0)[0:1, :]
    grad_rms = jnp.sqrt(square_sum / (groups * n_mp * span) + 1e-06)
    gf_ref[...] = raw * jnp.minimum(1.0, 1.0 / grad_rms)

    for i in range(PARTS):
        @pl.when(me > 0)
        def _():
            g_copy(i).wait_send()

        @pl.when(me < n_ctx - 1)
        def _():
            p_copy(i).wait_send()

    @pl.loop(1, n_ctx)
    def _(i):
        rs_copy(ctx_peer(i), me).wait_send()
        ag_copy(ctx_peer(i), me).wait_send()

    @pl.loop(1, n_mp)
    def _(i):
        sq_copy(mp_peer(i), slab).wait_send()


def shards(queries, key_feats, value_feats, filters, grad_out):
    n_ctx, n_mp = lax.axis_size("ctx"), lax.axis_size("mp")
    tokens, channels = queries.shape
    groups, span = filters.shape
    own = groups // n_ctx
    vmem = pl.BlockSpec(memory_space=pltpu.VMEM)
    dma = pltpu.SemaphoreType.DMA
    like = jax.ShapeDtypeStruct((tokens, channels), BF16)
    return pl.pallas_call(
        functools.partial(kernel, n_ctx, n_mp),
        out_shape=(like, like, like, like, jax.ShapeDtypeStruct((groups, span), F32)),
        in_specs=[vmem] * 5,
        out_specs=[vmem] * 5,
        scratch_shapes=[
            pltpu.VMEM((tokens, channels), BF16),
            pltpu.VMEM((tokens, channels), BF16),
            pltpu.VMEM((span, channels), BF16),
            pltpu.VMEM((span, channels), BF16),
            pltpu.VMEM((groups, span), F32),
            pltpu.VMEM((groups, span), F32),
            pltpu.VMEM((groups, span, 2 * span), BF16),
            pltpu.VMEM((groups, span, 2 * span), BF16),
            pltpu.VMEM((8 * groups, span), F32),
            pltpu.VMEM((n_ctx, own, span), F32),
            pltpu.VMEM((n_ctx, own, span), F32),
            pltpu.VMEM((own, span), F32),
            pltpu.VMEM((n_ctx, own, span), F32),
            pltpu.VMEM((8, span), F32),
            pltpu.VMEM((n_mp, 8, span), F32),
            dma((PARTS,)), dma((PARTS,)), dma((PARTS,)), dma((PARTS,)),
            dma((n_ctx,)), dma((n_ctx,)), dma((n_ctx,)), dma((n_ctx,)),
            dma((n_mp,)), dma((n_mp,)),
        ],
        compiler_params=pltpu.CompilerParams(
            collective_id=0, has_side_effects=True, vmem_limit_bytes=56 * 2**20),
    )(queries, key_feats, value_feats, filters, grad_out)


def solution(mesh):
    placed = (P("ctx", "mp"), P("ctx", "mp"), P("ctx", "mp"), P("mp", None), P("ctx", "mp"))
    return jax.shard_map(
        shards,
        mesh=mesh,
        in_specs=placed,
        out_specs=(P("ctx", "mp"), P("ctx", "mp"), P("ctx", "mp"), P("ctx", "mp"), P("mp", None)),
        check_vma=False,
    )
```

```python
import functools

import jax
import jax.numpy as jnp
from jax import lax
from jax.experimental import pallas as pl
from jax.experimental.pallas import tpu as pltpu
from jax.sharding import PartitionSpec as P

G = 16
MESH = pl.DeviceIdType.MESH
F32 = jnp.float32
BF16 = jnp.bfloat16
WIDE = 128
PARTS = 4


def times(a, b):
    return (a.astype(F32) * b.astype(F32)).astype(BF16)


def kernel(n_ctx, n_mp, q_ref, k_ref, v_ref, f_ref, g_ref,
           mix_ref, gq_ref, gk_ref, gv_ref, gf_ref,
           prod, gmix, phalo, ghalo, taps, flipped, toep, toep_f, folded,
           partial, arrived, reduced, gathered, own_sq, all_sq,
           p_send, p_recv, g_send, g_recv,
           rs_send, rs_recv, ag_send, ag_recv, sq_send, sq_recv):
    tokens, channels = q_ref.shape
    groups, span = f_ref.shape
    blocks = tokens // span
    own = groups // n_ctx
    part = channels // PARTS
    me = lax.axis_index("ctx")
    slab = lax.axis_index("mp")
    per_chunk = WIDE // G

    def ctx_peer(i):
        return lax.rem(me + i, n_ctx)

    def mp_peer(i):
        return lax.rem(slab + i, n_mp)

    barrier = pltpu.get_barrier_semaphore()

    @pl.loop(1, n_ctx)
    def _(i):
        pl.semaphore_signal(barrier, inc=1, device_id=(ctx_peer(i), slab), device_id_type=MESH)

    @pl.loop(1, n_mp)
    def _(i):
        pl.semaphore_signal(barrier, inc=1, device_id=(me, mp_peer(i)), device_id_type=MESH)

    head, tail = slice(0, span), slice(tokens - span, tokens)
    gmix[head, :] = times(g_ref[head, :], q_ref[head, :])
    prod[tail, :] = times(k_ref[tail, :], v_ref[tail, :])
    pl.semaphore_wait(barrier, n_ctx + n_mp - 2)

    def g_copy(i):
        cols = slice(i * part, (i + 1) * part)
        return pltpu.make_async_remote_copy(
            src_ref=gmix.at[head, cols], dst_ref=ghalo.at[:, cols],
            send_sem=g_send.at[i], recv_sem=g_recv.at[i],
            device_id=(lax.rem(me + n_ctx - 1, n_ctx), slab), device_id_type=MESH)

    def p_copy(i):
        cols = slice(i * part, (i + 1) * part)
        return pltpu.make_async_remote_copy(
            src_ref=prod.at[tail, cols], dst_ref=phalo.at[:, cols],
            send_sem=p_send.at[i], recv_sem=p_recv.at[i],
            device_id=(lax.rem(me + 1, n_ctx), slab), device_id_type=MESH)

    for i in range(PARTS):
        @pl.when(me > 0)
        def _():
            g_copy(i).start()

        @pl.when(me < n_ctx - 1)
        def _():
            p_copy(i).start()

    @pl.when(me == 0)
    def _():
        phalo[...] = jnp.zeros_like(phalo)

    @pl.when(me == n_ctx - 1)
    def _():
        ghalo[...] = jnp.zeros_like(ghalo)

    rest_g, rest_p = slice(span, tokens), slice(0, tokens - span)
    gmix[rest_g, :] = times(g_ref[rest_g, :], q_ref[rest_g, :])
    prod[rest_p, :] = times(k_ref[rest_p, :], v_ref[rest_p, :])
    taps[...] = f_ref[...].astype(F32)

    col = lax.broadcasted_iota(jnp.int32, (span, span), 1)
    row = lax.broadcasted_iota(jnp.int32, (span, span), 0)
    upper = col >= row

    flip = jnp.where(lax.rem(row + col, span) == 0, 1.0, 0.0).astype(BF16)
    flipped[...] = jnp.dot(f_ref[...], flip, preferred_element_type=F32)

    def spread(i, lines, out, mask):
        line = jnp.broadcast_to(lines[pl.ds(i, 1), :], (span, span))
        turned = pltpu.roll(line, 0, 1, stride=1, stride_axis=0)
        zero = jnp.zeros_like(turned)
        out[i, :, 0:span] = jnp.where(mask, turned, zero).astype(BF16)
        out[i, :, span:] = jnp.where(mask, zero, turned).astype(BF16)

    @pl.loop(0, groups // per_chunk)
    def _(c):
        for j in range(per_chunk):
            spread(c * per_chunk + j, taps, toep, upper)
            spread(c * per_chunk + j, flipped, toep_f, col > row)

    lane = lax.broadcasted_iota(jnp.int32, (1, blocks * WIDE), 1)
    member = lax.rem(lane, WIDE) // G

    def g_windows(at):
        own_part = gmix[:, at]
        last = jnp.concatenate([gmix[tail, at], ghalo[:, at]], axis=0)
        wins = [own_part[n * span:(n + 2) * span] for n in range(blocks - 1)]
        return jnp.concatenate(wins + [last], axis=1)

    def p_windows(at):
        own_part = prod[:, at]
        first = jnp.concatenate([phalo[:, at], prod[head, at]], axis=0)
        wins = [own_part[(n - 1) * span:(n + 1) * span] for n in range(1, blocks)]
        return jnp.concatenate([first] + wins, axis=1)

    def conv(c, mats, wins):
        stack = mats[pl.ds(pl.multiple_of(c * per_chunk, per_chunk), per_chunk)]
        y = jnp.dot(stack.reshape(per_chunk * span, 2 * span), wins,
                    preferred_element_type=F32)
        out = y[:span]
        for j in range(1, per_chunk):
            out = jnp.where(member == j, y[j * span:(j + 1) * span], out)
        out = out.astype(BF16)
        return jnp.concatenate(
            [out[:, n * WIDE:(n + 1) * WIDE] for n in range(blocks)], axis=0)

    @pl.when(me < n_ctx - 1)
    def _():
        for i in range(PARTS):
            g_copy(i).wait_recv()

    @pl.loop(0, channels // WIDE)
    def _(c):
        at = pl.ds(pl.multiple_of(c * WIDE, WIDE), WIDE)
        wins = g_windows(at).T
        left = jnp.concatenate(
            [prod[n * span:(n + 1) * span, at] for n in range(blocks)], axis=1)
        mine = jnp.concatenate(
            [jnp.where(member == j, left, jnp.zeros_like(left)) for j in range(per_chunk)], axis=0)
        every = jnp.dot(mine, wins, preferred_element_type=F32)
        for j in range(per_chunk):
            both = every[j * span:(j + 1) * span]
            turn = jnp.where(upper, both[:, :span], both[:, span:])
            half = span // 2
            while half >= 8:
                turn = turn[:half] + pltpu.roll(turn[half:], span - half, 1)
                half //= 2
            folded[pl.ds(pl.multiple_of((c * per_chunk + j) * 8, 8), 8), :] = turn

    total = folded[pl.ds(0, groups, stride=8), :]
    for r in range(1, 8):
        total = total + pltpu.roll(folded[pl.ds(r, groups, stride=8), :], span - r, 1)
    partial[...] = total.reshape(partial.shape)

    def rs_copy(to, sender):
        return pltpu.make_async_remote_copy(
            src_ref=partial.at[to], dst_ref=arrived.at[sender],
            send_sem=rs_send.at[to], recv_sem=rs_recv.at[sender],
            device_id=(to, slab), device_id_type=MESH)

    def ag_copy(to, sender):
        return pltpu.make_async_remote_copy(
            src_ref=reduced, dst_ref=gathered.at[sender],
            send_sem=ag_send.at[to], recv_sem=ag_recv.at[sender],
            device_id=(to, slab), device_id_type=MESH)

    def sq_copy(to, sender):
        return pltpu.make_async_remote_copy(
            src_ref=own_sq, dst_ref=all_sq.at[sender],
            send_sem=sq_send.at[to], recv_sem=sq_recv.at[sender],
            device_id=(me, to), device_id_type=MESH)

    @pl.loop(1, n_ctx)
    def _(i):
        rs_copy(ctx_peer(i), me).start()

    arrived[me] = partial[me]

    @pl.when(me > 0)
    def _():
        for i in range(PARTS):
            p_copy(i).wait_recv()

    def both_convs(c):
        at = pl.ds(pl.multiple_of(c * WIDE, WIDE), WIDE)
        back = conv(c, toep, g_windows(at))
        ahead = conv(c, toep_f, p_windows(at))
        gk_ref[:, at] = times(back, v_ref[:, at])
        gv_ref[:, at] = times(back, k_ref[:, at])
        mix_ref[:, at] = times(ahead, q_ref[:, at])
        gq_ref[:, at] = times(ahead, g_ref[:, at])

    chunks = channels // WIDE
    pl.loop(0, chunks // 2)(both_convs)

    @pl.loop(1, n_ctx)
    def _(i):
        rs_copy(me, ctx_peer(i)).wait_recv()

    reduced[...] = jnp.sum(arrived[...], axis=0)

    @pl.loop(1, n_ctx)
    def _(i):
        ag_copy(ctx_peer(i), me).start()

    gathered[me] = reduced[...]

    pl.loop(chunks // 2, chunks)(both_convs)

    @pl.loop(1, n_ctx)
    def _(i):
        ag_copy(me, ctx_peer(i)).wait_recv()

    raw = gathered[...].reshape(groups, span)
    squares = jnp.sum(jnp.sum(raw * raw, axis=0, keepdims=True), axis=1, keepdims=True)
    own_sq[...] = jnp.broadcast_to(squares, own_sq.shape)

    @pl.loop(1, n_mp)
    def _(i):
        sq_copy(mp_peer(i), slab).start()

    all_sq[slab] = own_sq[...]

    @pl.loop(1, n_mp)
    def _(i):
        sq_copy(slab, mp_peer(i)).wait_recv()

    square_sum = jnp.sum(all_sq[...], axis=0)[0:1, :]
    grad_rms = jnp.sqrt(square_sum / (groups * n_mp * span) + 1e-06)
    gf_ref[...] = raw * jnp.minimum(1.0, 1.0 / grad_rms)

    for i in range(PARTS):
        @pl.when(me > 0)
        def _():
            g_copy(i).wait_send()

        @pl.when(me < n_ctx - 1)
        def _():
            p_copy(i).wait_send()

    @pl.loop(1, n_ctx)
    def _(i):
        rs_copy(ctx_peer(i), me).wait_send()
        ag_copy(ctx_peer(i), me).wait_send()

    @pl.loop(1, n_mp)
    def _(i):
        sq_copy(mp_peer(i), slab).wait_send()


def shards(queries, key_feats, value_feats, filters, grad_out):
    n_ctx, n_mp = lax.axis_size("ctx"), lax.axis_size("mp")
    tokens, channels = queries.shape
    groups, span = filters.shape
    own = groups // n_ctx
    vmem = pl.BlockSpec(memory_space=pltpu.VMEM)
    dma = pltpu.SemaphoreType.DMA
    like = jax.ShapeDtypeStruct((tokens, channels), BF16)
    return pl.pallas_call(
        functools.partial(kernel, n_ctx, n_mp),
        out_shape=(like, like, like, like, jax.ShapeDtypeStruct((groups, span), F32)),
        in_specs=[vmem] * 5,
        out_specs=[vmem] * 5,
        scratch_shapes=[
            pltpu.VMEM((tokens, channels), BF16),
            pltpu.VMEM((tokens, channels), BF16),
            pltpu.VMEM((span, channels), BF16),
            pltpu.VMEM((span, channels), BF16),
            pltpu.VMEM((groups, span), F32),
            pltpu.VMEM((groups, span), F32),
            pltpu.VMEM((groups, span, 2 * span), BF16),
            pltpu.VMEM((groups, span, 2 * span), BF16),
            pltpu.VMEM((8 * groups, span), F32),
            pltpu.VMEM((n_ctx, own, span), F32),
            pltpu.VMEM((n_ctx, own, span), F32),
            pltpu.VMEM((own, span), F32),
            pltpu.VMEM((n_ctx, own, span), F32),
            pltpu.VMEM((8, span), F32),
            pltpu.VMEM((n_mp, 8, span), F32),
            dma((PARTS,)), dma((PARTS,)), dma((PARTS,)), dma((PARTS,)),
            dma((n_ctx,)), dma((n_ctx,)), dma((n_ctx,)), dma((n_ctx,)),
            dma((n_mp,)), dma((n_mp,)),
        ],
        compiler_params=pltpu.CompilerParams(
            collective_id=0, has_side_effects=True, vmem_limit_bytes=56 * 2**20),
    )(queries, key_feats, value_feats, filters, grad_out)


def solution(mesh):
    placed = (P("ctx", "mp"), P("ctx", "mp"), P("ctx", "mp"), P("mp", None), P("ctx", "mp"))
    return jax.shard_map(
        shards,
        mesh=mesh,
        in_specs=placed,
        out_specs=(P("ctx", "mp"), P("ctx", "mp"), P("ctx", "mp"), P("ctx", "mp"), P("mp", None)),
        check_vma=False,
    )
```

```python
import functools

import jax
import jax.numpy as jnp
from jax import lax
from jax.experimental import pallas as pl
from jax.experimental.pallas import tpu as pltpu
from jax.sharding import PartitionSpec as P

G = 16
MESH = pl.DeviceIdType.MESH
F32 = jnp.float32
BF16 = jnp.bfloat16
WIDE = 128
PARTS = 4


def times(a, b):
    return (a.astype(F32) * b.astype(F32)).astype(BF16)


def kernel(n_ctx, n_mp, q_ref, k_ref, v_ref, f_ref, g_ref,
           mix_ref, gq_ref, gk_ref, gv_ref, gf_ref,
           prod, gmix, phalo, ghalo, taps, flipped, toep, toep_f, folded,
           partial, arrived, reduced, gathered, own_sq, all_sq,
           p_send, p_recv, g_send, g_recv,
           rs_send, rs_recv, ag_send, ag_recv, sq_send, sq_recv):
    tokens, channels = q_ref.shape
    groups, span = f_ref.shape
    blocks = tokens // span
    own = groups // n_ctx
    part = channels // PARTS
    me = lax.axis_index("ctx")
    slab = lax.axis_index("mp")
    per_chunk = WIDE // G

    def ctx_peer(i):
        return lax.rem(me + i, n_ctx)

    def mp_peer(i):
        return lax.rem(slab + i, n_mp)

    barrier = pltpu.get_barrier_semaphore()

    @pl.loop(1, n_ctx)
    def _(i):
        pl.semaphore_signal(barrier, inc=1, device_id=(ctx_peer(i), slab), device_id_type=MESH)

    @pl.loop(1, n_mp)
    def _(i):
        pl.semaphore_signal(barrier, inc=1, device_id=(me, mp_peer(i)), device_id_type=MESH)

    head, tail = slice(0, span), slice(tokens - span, tokens)
    gmix[head, :] = times(g_ref[head, :], q_ref[head, :])
    prod[tail, :] = times(k_ref[tail, :], v_ref[tail, :])
    pl.semaphore_wait(barrier, n_ctx + n_mp - 2)

    def g_copy(i):
        cols = slice(i * part, (i + 1) * part)
        return pltpu.make_async_remote_copy(
            src_ref=gmix.at[head, cols], dst_ref=ghalo.at[:, cols],
            send_sem=g_send.at[i], recv_sem=g_recv.at[i],
            device_id=(lax.rem(me + n_ctx - 1, n_ctx), slab), device_id_type=MESH)

    def p_copy(i):
        cols = slice(i * part, (i + 1) * part)
        return pltpu.make_async_remote_copy(
            src_ref=prod.at[tail, cols], dst_ref=phalo.at[:, cols],
            send_sem=p_send.at[i], recv_sem=p_recv.at[i],
            device_id=(lax.rem(me + 1, n_ctx), slab), device_id_type=MESH)

    for i in range(PARTS):
        @pl.when(me > 0)
        def _():
            g_copy(i).start()

        @pl.when(me < n_ctx - 1)
        def _():
            p_copy(i).start()

    @pl.when(me == 0)
    def _():
        phalo[...] = jnp.zeros_like(phalo)

    @pl.when(me == n_ctx - 1)
    def _():
        ghalo[...] = jnp.zeros_like(ghalo)

    rest_g, rest_p = slice(span, tokens), slice(0, tokens - span)
    gmix[rest_g, :] = times(g_ref[rest_g, :], q_ref[rest_g, :])
    prod[rest_p, :] = times(k_ref[rest_p, :], v_ref[rest_p, :])
    taps[...] = f_ref[...].astype(F32)

    col = lax.broadcasted_iota(jnp.int32, (span, span), 1)
    row = lax.broadcasted_iota(jnp.int32, (span, span), 0)
    upper = col >= row

    flip = jnp.where(lax.rem(row + col, span) == 0, 1.0, 0.0).astype(BF16)
    flipped[...] = jnp.dot(f_ref[...], flip, preferred_element_type=F32)

    def spread(i, lines, out, mask):
        line = jnp.broadcast_to(lines[pl.ds(i, 1), :], (span, span))
        turned = pltpu.roll(line, 0, 1, stride=1, stride_axis=0)
        zero = jnp.zeros_like(turned)
        out[i, :, 0:span] = jnp.where(mask, turned, zero).astype(BF16)
        out[i, :, span:] = jnp.where(mask, zero, turned).astype(BF16)

    @pl.loop(0, groups // per_chunk)
    def _(c):
        for j in range(per_chunk):
            spread(c * per_chunk + j, taps, toep, upper)
            spread(c * per_chunk + j, flipped, toep_f, col > row)

    lane = lax.broadcasted_iota(jnp.int32, (1, blocks * WIDE), 1)
    member = lax.rem(lane, WIDE) // G

    def g_windows(at):
        own_part = gmix[:, at]
        last = jnp.concatenate([gmix[tail, at], ghalo[:, at]], axis=0)
        wins = [own_part[n * span:(n + 2) * span] for n in range(blocks - 1)]
        return jnp.concatenate(wins + [last], axis=1)

    def p_windows(at):
        own_part = prod[:, at]
        first = jnp.concatenate([phalo[:, at], prod[head, at]], axis=0)
        wins = [own_part[(n - 1) * span:(n + 1) * span] for n in range(1, blocks)]
        return jnp.concatenate([first] + wins, axis=1)

    def conv(c, mats, wins):
        stack = mats[pl.ds(pl.multiple_of(c * per_chunk, per_chunk), per_chunk)]
        y = jnp.dot(stack.reshape(per_chunk * span, 2 * span), wins,
                    preferred_element_type=F32).astype(BF16)
        out = y[:span]
        for j in range(1, per_chunk):
            out = jnp.where(member == j, y[j * span:(j + 1) * span], out)
        return jnp.concatenate(
            [out[:, n * WIDE:(n + 1) * WIDE] for n in range(blocks)], axis=0)

    @pl.when(me < n_ctx - 1)
    def _():
        for i in range(PARTS):
            g_copy(i).wait_recv()

    @pl.loop(0, channels // WIDE)
    def _(c):
        at = pl.ds(pl.multiple_of(c * WIDE, WIDE), WIDE)
        wins = g_windows(at).T
        left = jnp.concatenate(
            [prod[n * span:(n + 1) * span, at] for n in range(blocks)], axis=1)
        mine = jnp.concatenate(
            [jnp.where(member == j, left, jnp.zeros_like(left)) for j in range(per_chunk)], axis=0)
        every = jnp.dot(mine, wins, preferred_element_type=F32)
        for j in range(per_chunk):
            both = every[j * span:(j + 1) * span]
            turn = jnp.where(upper, both[:, :span], both[:, span:])
            half = span // 2
            while half >= 8:
                turn = turn[:half] + pltpu.roll(turn[half:], span - half, 1)
                half //= 2
            folded[pl.ds(pl.multiple_of((c * per_chunk + j) * 8, 8), 8), :] = turn

    total = folded[pl.ds(0, groups, stride=8), :]
    for r in range(1, 8):
        total = total + pltpu.roll(folded[pl.ds(r, groups, stride=8), :], span - r, 1)
    partial[...] = total.reshape(partial.shape)

    def rs_copy(to, sender):
        return pltpu.make_async_remote_copy(
            src_ref=partial.at[to], dst_ref=arrived.at[sender],
            send_sem=rs_send.at[to], recv_sem=rs_recv.at[sender],
            device_id=(to, slab), device_id_type=MESH)

    def ag_copy(to, sender):
        return pltpu.make_async_remote_copy(
            src_ref=reduced, dst_ref=gathered.at[sender],
            send_sem=ag_send.at[to], recv_sem=ag_recv.at[sender],
            device_id=(to, slab), device_id_type=MESH)

    def sq_copy(to, sender):
        return pltpu.make_async_remote_copy(
            src_ref=own_sq, dst_ref=all_sq.at[sender],
            send_sem=sq_send.at[to], recv_sem=sq_recv.at[sender],
            device_id=(me, to), device_id_type=MESH)

    @pl.loop(1, n_ctx)
    def _(i):
        rs_copy(ctx_peer(i), me).start()

    arrived[me] = partial[me]

    @pl.when(me > 0)
    def _():
        for i in range(PARTS):
            p_copy(i).wait_recv()

    def both_convs(c):
        at = pl.ds(pl.multiple_of(c * WIDE, WIDE), WIDE)
        back = conv(c, toep, g_windows(at))
        ahead = conv(c, toep_f, p_windows(at))
        gk_ref[:, at] = times(back, v_ref[:, at])
        gv_ref[:, at] = times(back, k_ref[:, at])
        mix_ref[:, at] = times(ahead, q_ref[:, at])
        gq_ref[:, at] = times(ahead, g_ref[:, at])

    chunks = channels // WIDE
    pl.loop(0, chunks // 2)(both_convs)

    @pl.loop(1, n_ctx)
    def _(i):
        rs_copy(me, ctx_peer(i)).wait_recv()

    reduced[...] = jnp.sum(arrived[...], axis=0)

    @pl.loop(1, n_ctx)
    def _(i):
        ag_copy(ctx_peer(i), me).start()

    gathered[me] = reduced[...]

    pl.loop(chunks // 2, chunks)(both_convs)

    @pl.loop(1, n_ctx)
    def _(i):
        ag_copy(me, ctx_peer(i)).wait_recv()

    raw = gathered[...].reshape(groups, span)
    squares = jnp.sum(jnp.sum(raw * raw, axis=0, keepdims=True), axis=1, keepdims=True)
    own_sq[...] = jnp.broadcast_to(squares, own_sq.shape)

    @pl.loop(1, n_mp)
    def _(i):
        sq_copy(mp_peer(i), slab).start()

    all_sq[slab] = own_sq[...]

    @pl.loop(1, n_mp)
    def _(i):
        sq_copy(slab, mp_peer(i)).wait_recv()

    square_sum = jnp.sum(all_sq[...], axis=0)[0:1, :]
    grad_rms = jnp.sqrt(square_sum / (groups * n_mp * span) + 1e-06)
    gf_ref[...] = raw * jnp.minimum(1.0, 1.0 / grad_rms)

    for i in range(PARTS):
        @pl.when(me > 0)
        def _():
            g_copy(i).wait_send()

        @pl.when(me < n_ctx - 1)
        def _():
            p_copy(i).wait_send()

    @pl.loop(1, n_ctx)
    def _(i):
        rs_copy(ctx_peer(i), me).wait_send()
        ag_copy(ctx_peer(i), me).wait_send()

    @pl.loop(1, n_mp)
    def _(i):
        sq_copy(mp_peer(i), slab).wait_send()


def shards(queries, key_feats, value_feats, filters, grad_out):
    n_ctx, n_mp = lax.axis_size("ctx"), lax.axis_size("mp")
    tokens, channels = queries.shape
    groups, span = filters.shape
    own = groups // n_ctx
    vmem = pl.BlockSpec(memory_space=pltpu.VMEM)
    dma = pltpu.SemaphoreType.DMA
    like = pltpu.VMEM((tokens, channels), BF16)
    return pl.pallas_call(
        functools.partial(kernel, n_ctx, n_mp),
        out_shape=(like, like, like, like, pltpu.VMEM((groups, span), F32)),
        in_specs=[vmem] * 5,
        out_specs=[vmem] * 5,
        scratch_shapes=[
            pltpu.VMEM((tokens, channels), BF16),
            pltpu.VMEM((tokens, channels), BF16),
            pltpu.VMEM((span, channels), BF16),
            pltpu.VMEM((span, channels), BF16),
            pltpu.VMEM((groups, span), F32),
            pltpu.VMEM((groups, span), F32),
            pltpu.VMEM((groups, span, 2 * span), BF16),
            pltpu.VMEM((groups, span, 2 * span), BF16),
            pltpu.VMEM((8 * groups, span), F32),
            pltpu.VMEM((n_ctx, own, span), F32),
            pltpu.VMEM((n_ctx, own, span), F32),
            pltpu.VMEM((own, span), F32),
            pltpu.VMEM((n_ctx, own, span), F32),
            pltpu.VMEM((8, span), F32),
            pltpu.VMEM((n_mp, 8, span), F32),
            dma((PARTS,)), dma((PARTS,)), dma((PARTS,)), dma((PARTS,)),
            dma((n_ctx,)), dma((n_ctx,)), dma((n_ctx,)), dma((n_ctx,)),
            dma((n_mp,)), dma((n_mp,)),
        ],
        compiler_params=pltpu.CompilerParams(
            collective_id=0, has_side_effects=True, vmem_limit_bytes=56 * 2**20),
    )(queries, key_feats, value_feats, filters, grad_out)


def solution(mesh):
    placed = (P("ctx", "mp"), P("ctx", "mp"), P("ctx", "mp"), P("mp", None), P("ctx", "mp"))
    return jax.shard_map(
        shards,
        mesh=mesh,
        in_specs=placed,
        out_specs=(P("ctx", "mp"), P("ctx", "mp"), P("ctx", "mp"), P("ctx", "mp"), P("mp", None)),
        check_vma=False,
    )
```

```python
import functools

import jax
import jax.numpy as jnp
from jax import lax
from jax.experimental import pallas as pl
from jax.experimental.pallas import tpu as pltpu
from jax.sharding import PartitionSpec as P

G = 16
MESH = pl.DeviceIdType.MESH
F32 = jnp.float32
BF16 = jnp.bfloat16
WIDE = 128
PART = 256


def times(a, b):
    return (a.astype(F32) * b.astype(F32)).astype(BF16)


def kernel(n_ctx, n_mp, q_hbm, k_hbm, v_hbm, f_ref, g_hbm,
           mix_ref, gq_ref, gk_ref, gv_ref, gf_ref,
           q_ref, k_ref, v_ref, g_ref, prod, gmix, phalo, ghalo, taps, flipped, toep, toep_f, folded,
           partial, arrived, reduced, gathered, own_sq, all_sq,
           p_send, p_recv, g_send, g_recv,
           rs_send, rs_recv, ag_send, ag_recv, sq_send, sq_recv, load):
    tokens, channels = q_ref.shape
    groups, span = f_ref.shape
    blocks = tokens // span
    own = groups // n_ctx
    parts = channels // PART
    me = lax.axis_index("ctx")
    slab = lax.axis_index("mp")
    per_chunk = WIDE // G

    def ctx_peer(i):
        return lax.rem(me + i, n_ctx)

    def mp_peer(i):
        return lax.rem(slab + i, n_mp)

    barrier = pltpu.get_barrier_semaphore()

    @pl.loop(1, n_ctx)
    def _(i):
        pl.semaphore_signal(barrier, inc=1, device_id=(ctx_peer(i), slab), device_id_type=MESH)

    @pl.loop(1, n_mp)
    def _(i):
        pl.semaphore_signal(barrier, inc=1, device_id=(me, mp_peer(i)), device_id_type=MESH)

    head, tail = slice(0, span), slice(tokens - span, tokens)
    rest_g, rest_p = slice(span, tokens), slice(0, tokens - span)

    def loads(pairs, first):
        return [pltpu.make_async_copy(a.at[rows, :], b.at[rows, :], load.at[first + i])
                for i, (a, b, rows) in enumerate(pairs)]

    edges = loads([(g_hbm, g_ref, head), (q_hbm, q_ref, head),
                   (k_hbm, k_ref, tail), (v_hbm, v_ref, tail)], 0)
    others = loads([(g_hbm, g_ref, rest_g), (q_hbm, q_ref, rest_g),
                    (k_hbm, k_ref, rest_p), (v_hbm, v_ref, rest_p)], 4)
    for copy in edges + others:
        copy.start()
    for copy in edges:
        copy.wait()
    gmix[head, :] = times(g_ref[head, :], q_ref[head, :])
    prod[tail, :] = times(k_ref[tail, :], v_ref[tail, :])
    pl.semaphore_wait(barrier, n_ctx + n_mp - 2)

    def g_copy(i):
        cols = pl.ds(pl.multiple_of(i * PART, PART), PART)
        return pltpu.make_async_remote_copy(
            src_ref=gmix.at[head, cols], dst_ref=ghalo.at[:, cols],
            send_sem=g_send.at[i], recv_sem=g_recv.at[i],
            device_id=(lax.rem(me + n_ctx - 1, n_ctx), slab), device_id_type=MESH)

    def p_copy(i):
        cols = pl.ds(pl.multiple_of(i * PART, PART), PART)
        return pltpu.make_async_remote_copy(
            src_ref=prod.at[tail, cols], dst_ref=phalo.at[:, cols],
            send_sem=p_send.at[i], recv_sem=p_recv.at[i],
            device_id=(lax.rem(me + 1, n_ctx), slab), device_id_type=MESH)

    @pl.loop(0, parts)
    def _(i):
        @pl.when(me > 0)
        def _():
            g_copy(i).start()

        @pl.when(me < n_ctx - 1)
        def _():
            p_copy(i).start()

    @pl.when(me == 0)
    def _():
        phalo[...] = jnp.zeros_like(phalo)

    @pl.when(me == n_ctx - 1)
    def _():
        ghalo[...] = jnp.zeros_like(ghalo)

    for copy in others:
        copy.wait()
    gmix[rest_g, :] = times(g_ref[rest_g, :], q_ref[rest_g, :])
    prod[rest_p, :] = times(k_ref[rest_p, :], v_ref[rest_p, :])
    taps[...] = f_ref[...].astype(F32)

    col = lax.broadcasted_iota(jnp.int32, (span, span), 1)
    row = lax.broadcasted_iota(jnp.int32, (span, span), 0)
    upper = col >= row

    flip = jnp.where(lax.rem(row + col, span) == 0, 1.0, 0.0).astype(BF16)
    flipped[...] = jnp.dot(f_ref[...], flip, preferred_element_type=F32)

    def spread(i, lines, out, mask):
        line = jnp.broadcast_to(lines[pl.ds(i, 1), :], (span, span))
        turned = pltpu.roll(line, 0, 1, stride=1, stride_axis=0)
        zero = jnp.zeros_like(turned)
        out[i, :, 0:span] = jnp.where(mask, turned, zero).astype(BF16)
        out[i, :, span:] = jnp.where(mask, zero, turned).astype(BF16)

    @pl.loop(0, groups // per_chunk)
    def _(c):
        for j in range(per_chunk):
            spread(c * per_chunk + j, taps, toep, upper)
            spread(c * per_chunk + j, flipped, toep_f, col > row)

    lane = lax.broadcasted_iota(jnp.int32, (1, blocks * WIDE), 1)
    member = lax.rem(lane, WIDE) // G

    def g_windows(at):
        own_part = gmix[:, at]
        last = jnp.concatenate([gmix[tail, at], ghalo[:, at]], axis=0)
        wins = [own_part[n * span:(n + 2) * span] for n in range(blocks - 1)]
        return jnp.concatenate(wins + [last], axis=1)

    def p_windows(at):
        own_part = prod[:, at]
        first = jnp.concatenate([phalo[:, at], prod[head, at]], axis=0)
        wins = [own_part[(n - 1) * span:(n + 1) * span] for n in range(1, blocks)]
        return jnp.concatenate([first] + wins, axis=1)

    def conv(c, mats, wins):
        stack = mats[pl.ds(pl.multiple_of(c * per_chunk, per_chunk), per_chunk)]
        y = jnp.dot(stack.reshape(per_chunk * span, 2 * span), wins,
                    preferred_element_type=F32).astype(BF16)
        out = y[:span]
        for j in range(1, per_chunk):
            out = jnp.where(member == j, y[j * span:(j + 1) * span], out)
        return jnp.concatenate(
            [out[:, n * WIDE:(n + 1) * WIDE] for n in range(blocks)], axis=0)

    chunks = PART // WIDE

    def correlate(c):
        at = pl.ds(pl.multiple_of(c * WIDE, WIDE), WIDE)
        wins = g_windows(at).T
        left = jnp.concatenate(
            [prod[n * span:(n + 1) * span, at] for n in range(blocks)], axis=1)
        mine = jnp.concatenate(
            [jnp.where(member == j, left, jnp.zeros_like(left)) for j in range(per_chunk)], axis=0)
        every = jnp.dot(mine, wins, preferred_element_type=F32)
        for j in range(per_chunk):
            both = every[j * span:(j + 1) * span]
            turn = jnp.where(upper, both[:, :span], both[:, span:])
            half = span // 2
            while half >= 8:
                turn = turn[:half] + pltpu.roll(turn[half:], span - half, 1)
                half //= 2
            folded[pl.ds(pl.multiple_of((c * per_chunk + j) * 8, 8), 8), :] = turn

    @pl.loop(0, parts)
    def _(i):
        @pl.when(me < n_ctx - 1)
        def _():
            g_copy(i).wait_recv()

        for c in range(chunks):
            correlate(i * chunks + c)

    total = folded[pl.ds(0, groups, stride=8), :]
    for r in range(1, 8):
        total = total + pltpu.roll(folded[pl.ds(r, groups, stride=8), :], span - r, 1)
    partial[...] = total.reshape(partial.shape)

    def rs_copy(to, sender):
        return pltpu.make_async_remote_copy(
            src_ref=partial.at[to], dst_ref=arrived.at[sender],
            send_sem=rs_send.at[to], recv_sem=rs_recv.at[sender],
            device_id=(to, slab), device_id_type=MESH)

    def ag_copy(to, sender):
        return pltpu.make_async_remote_copy(
            src_ref=reduced, dst_ref=gathered.at[sender],
            send_sem=ag_send.at[to], recv_sem=ag_recv.at[sender],
            device_id=(to, slab), device_id_type=MESH)

    def sq_copy(to, sender):
        return pltpu.make_async_remote_copy(
            src_ref=own_sq, dst_ref=all_sq.at[sender],
            send_sem=sq_send.at[to], recv_sem=sq_recv.at[sender],
            device_id=(me, to), device_id_type=MESH)

    @pl.loop(1, n_ctx)
    def _(i):
        rs_copy(ctx_peer(i), me).start()

    arrived[me] = partial[me]

    def both_convs(c):
        at = pl.ds(pl.multiple_of(c * WIDE, WIDE), WIDE)
        back = conv(c, toep, g_windows(at))
        ahead = conv(c, toep_f, p_windows(at))
        gk_ref[:, at] = times(back, v_ref[:, at])
        gv_ref[:, at] = times(back, k_ref[:, at])
        mix_ref[:, at] = times(ahead, q_ref[:, at])
        gq_ref[:, at] = times(ahead, g_ref[:, at])

    def convs(i):
        @pl.when(me > 0)
        def _():
            p_copy(i).wait_recv()

        for c in range(chunks):
            both_convs(i * chunks + c)

    pl.loop(0, parts // 2)(convs)

    @pl.loop(1, n_ctx)
    def _(i):
        rs_copy(me, ctx_peer(i)).wait_recv()

    reduced[...] = jnp.sum(arrived[...], axis=0)

    @pl.loop(1, n_ctx)
    def _(i):
        ag_copy(ctx_peer(i), me).start()

    gathered[me] = reduced[...]

    pl.loop(parts // 2, parts)(convs)

    @pl.loop(1, n_ctx)
    def _(i):
        ag_copy(me, ctx_peer(i)).wait_recv()

    raw = gathered[...].reshape(groups, span)
    squares = jnp.sum(jnp.sum(raw * raw, axis=0, keepdims=True), axis=1, keepdims=True)
    own_sq[...] = jnp.broadcast_to(squares, own_sq.shape)

    @pl.loop(1, n_mp)
    def _(i):
        sq_copy(mp_peer(i), slab).start()

    all_sq[slab] = own_sq[...]

    @pl.loop(1, n_mp)
    def _(i):
        sq_copy(slab, mp_peer(i)).wait_recv()

    square_sum = jnp.sum(all_sq[...], axis=0)[0:1, :]
    grad_rms = jnp.sqrt(square_sum / (groups * n_mp * span) + 1e-06)
    gf_ref[...] = raw * jnp.minimum(1.0, 1.0 / grad_rms)

    @pl.loop(0, parts)
    def _(i):
        @pl.when(me > 0)
        def _():
            g_copy(i).wait_send()

        @pl.when(me < n_ctx - 1)
        def _():
            p_copy(i).wait_send()

    @pl.loop(1, n_ctx)
    def _(i):
        rs_copy(ctx_peer(i), me).wait_send()
        ag_copy(ctx_peer(i), me).wait_send()

    @pl.loop(1, n_mp)
    def _(i):
        sq_copy(mp_peer(i), slab).wait_send()


def unload(a, b, c, d, e, ao, bo, co, do, eo, sems):
    copies = [pltpu.make_async_copy(x, y, sems.at[i]) for i, (x, y) in enumerate(
        zip((a, b, c, d, e), (ao, bo, co, do, eo)))]
    for copy in copies:
        copy.start()
    for copy in copies:
        copy.wait()


def shards(queries, key_feats, value_feats, filters, grad_out):
    n_ctx, n_mp = lax.axis_size("ctx"), lax.axis_size("mp")
    tokens, channels = queries.shape
    groups, span = filters.shape
    own = groups // n_ctx
    vmem = pl.BlockSpec(memory_space=pltpu.VMEM)
    dma = pltpu.SemaphoreType.DMA
    like = pltpu.VMEM((tokens, channels), BF16)
    anywhere = pl.BlockSpec(memory_space=pl.ANY)
    parts = channels // PART
    results = pl.pallas_call(
        functools.partial(kernel, n_ctx, n_mp),
        out_shape=(like, like, like, like, pltpu.VMEM((groups, span), F32)),
        in_specs=[anywhere] * 3 + [vmem, anywhere],
        out_specs=[vmem] * 5,
        scratch_shapes=[
            pltpu.VMEM((tokens, channels), BF16),
            pltpu.VMEM((tokens, channels), BF16),
            pltpu.VMEM((tokens, channels), BF16),
            pltpu.VMEM((tokens, channels), BF16),
            pltpu.VMEM((tokens, channels), BF16),
            pltpu.VMEM((tokens, channels), BF16),
            pltpu.VMEM((span, channels), BF16),
            pltpu.VMEM((span, channels), BF16),
            pltpu.VMEM((groups, span), F32),
            pltpu.VMEM((groups, span), F32),
            pltpu.VMEM((groups, span, 2 * span), BF16),
            pltpu.VMEM((groups, span, 2 * span), BF16),
            pltpu.VMEM((8 * groups, span), F32),
            pltpu.VMEM((n_ctx, own, span), F32),
            pltpu.VMEM((n_ctx, own, span), F32),
            pltpu.VMEM((own, span), F32),
            pltpu.VMEM((n_ctx, own, span), F32),
            pltpu.VMEM((8, span), F32),
            pltpu.VMEM((n_mp, 8, span), F32),
            dma((parts,)), dma((parts,)), dma((parts,)), dma((parts,)),
            dma((n_ctx,)), dma((n_ctx,)), dma((n_ctx,)), dma((n_ctx,)),
            dma((n_mp,)), dma((n_mp,)), dma((8,)),
        ],
        compiler_params=pltpu.CompilerParams(
            collective_id=0, has_side_effects=True, vmem_limit_bytes=56 * 2**20),
    )(queries, key_feats, value_feats, filters, grad_out)
    return pl.pallas_call(
        unload,
        out_shape=tuple(jax.ShapeDtypeStruct(x.shape, x.dtype) for x in results),
        in_specs=[vmem] * 5,
        out_specs=[anywhere] * 5,
        scratch_shapes=[dma((5,))],
    )(*results)


def solution(mesh):
    placed = (P("ctx", "mp"), P("ctx", "mp"), P("ctx", "mp"), P("mp", None), P("ctx", "mp"))
    return jax.shard_map(
        shards,
        mesh=mesh,
        in_specs=placed,
        out_specs=(P("ctx", "mp"), P("ctx", "mp"), P("ctx", "mp"), P("ctx", "mp"), P("mp", None)),
        check_vma=False,
    )
```

```python
import functools

import jax
import jax.numpy as jnp
from jax import lax
from jax.experimental import pallas as pl
from jax.experimental.pallas import tpu as pltpu
from jax.sharding import PartitionSpec as P

G = 16
MESH = pl.DeviceIdType.MESH
F32 = jnp.float32
BF16 = jnp.bfloat16
WIDE = 128
PART = 256


def times(a, b):
    return (a.astype(F32) * b.astype(F32)).astype(BF16)


def kernel(n_ctx, n_mp, q_hbm, k_hbm, v_hbm, f_ref, g_hbm,
           mix_ref, gq_ref, gk_ref, gv_ref, gf_ref,
           q_ref, k_ref, v_ref, g_ref, prod, gmix, phalo, ghalo, taps, flipped, toep, toep_f, folded,
           partial, arrived, reduced, gathered, own_sq, all_sq,
           p_send, p_recv, g_send, g_recv,
           rs_send, rs_recv, ag_send, ag_recv, sq_send, sq_recv, load):
    tokens, channels = q_ref.shape
    groups, span = f_ref.shape
    blocks = tokens // span
    own = groups // n_ctx
    parts = channels // PART
    me = lax.axis_index("ctx")
    slab = lax.axis_index("mp")
    per_chunk = WIDE // G

    def ctx_peer(i):
        return lax.rem(me + i, n_ctx)

    def mp_peer(i):
        return lax.rem(slab + i, n_mp)

    barrier = pltpu.get_barrier_semaphore()

    @pl.loop(1, n_ctx)
    def _(i):
        pl.semaphore_signal(barrier, inc=1, device_id=(ctx_peer(i), slab), device_id_type=MESH)

    @pl.loop(1, n_mp)
    def _(i):
        pl.semaphore_signal(barrier, inc=1, device_id=(me, mp_peer(i)), device_id_type=MESH)

    head, tail = slice(0, span), slice(tokens - span, tokens)
    rest_g, rest_p = slice(span, tokens), slice(0, tokens - span)

    def loads(pairs, first):
        return [pltpu.make_async_copy(a.at[rows, :], b.at[rows, :], load.at[first + i])
                for i, (a, b, rows) in enumerate(pairs)]

    edges = loads([(g_hbm, g_ref, head), (q_hbm, q_ref, head)], 0)
    others = loads([(k_hbm, k_ref, tail), (v_hbm, v_ref, tail),
                    (g_hbm, g_ref, rest_g), (q_hbm, q_ref, rest_g),
                    (k_hbm, k_ref, rest_p), (v_hbm, v_ref, rest_p)], 2)
    for copy in edges + others:
        copy.start()
    for copy in edges:
        copy.wait()
    gmix[head, :] = times(g_ref[head, :], q_ref[head, :])
    pl.semaphore_wait(barrier, n_ctx + n_mp - 2)

    def g_copy(i):
        cols = pl.ds(pl.multiple_of(i * PART, PART), PART)
        return pltpu.make_async_remote_copy(
            src_ref=gmix.at[head, cols], dst_ref=ghalo.at[:, cols],
            send_sem=g_send.at[i], recv_sem=g_recv.at[i],
            device_id=(lax.rem(me + n_ctx - 1, n_ctx), slab), device_id_type=MESH)

    def p_copy(i):
        cols = pl.ds(pl.multiple_of(i * PART, PART), PART)
        return pltpu.make_async_remote_copy(
            src_ref=prod.at[tail, cols], dst_ref=phalo.at[:, cols],
            send_sem=p_send.at[i], recv_sem=p_recv.at[i],
            device_id=(lax.rem(me + 1, n_ctx), slab), device_id_type=MESH)

    @pl.loop(0, parts)
    def _(i):
        @pl.when(me > 0)
        def _():
            g_copy(i).start()

    @pl.when(me == 0)
    def _():
        phalo[...] = jnp.zeros_like(phalo)

    @pl.when(me == n_ctx - 1)
    def _():
        ghalo[...] = jnp.zeros_like(ghalo)

    for copy in others:
        copy.wait()
    gmix[rest_g, :] = times(g_ref[rest_g, :], q_ref[rest_g, :])
    prod[...] = times(k_ref[...], v_ref[...])
    taps[...] = f_ref[...].astype(F32)

    col = lax.broadcasted_iota(jnp.int32, (span, span), 1)
    row = lax.broadcasted_iota(jnp.int32, (span, span), 0)
    upper = col >= row

    flip = jnp.where(lax.rem(row + col, span) == 0, 1.0, 0.0).astype(BF16)
    flipped[...] = jnp.dot(f_ref[...], flip, preferred_element_type=F32)

    def spread(i, lines, out, mask):
        line = jnp.broadcast_to(lines[pl.ds(i, 1), :], (span, span))
        turned = pltpu.roll(line, 0, 1, stride=1, stride_axis=0)
        zero = jnp.zeros_like(turned)
        out[i, :, 0:span] = jnp.where(mask, turned, zero).astype(BF16)
        out[i, :, span:] = jnp.where(mask, zero, turned).astype(BF16)

    @pl.loop(0, groups // per_chunk)
    def _(c):
        for j in range(per_chunk):
            spread(c * per_chunk + j, taps, toep, upper)
            spread(c * per_chunk + j, flipped, toep_f, col > row)

    @pl.loop(0, parts)
    def _(i):
        @pl.when(me < n_ctx - 1)
        def _():
            p_copy(i).start()

    lane = lax.broadcasted_iota(jnp.int32, (1, blocks * WIDE), 1)
    member = lax.rem(lane, WIDE) // G

    def g_windows(at):
        own_part = gmix[:, at]
        last = jnp.concatenate([gmix[tail, at], ghalo[:, at]], axis=0)
        wins = [own_part[n * span:(n + 2) * span] for n in range(blocks - 1)]
        return jnp.concatenate(wins + [last], axis=1)

    def p_windows(at):
        own_part = prod[:, at]
        first = jnp.concatenate([phalo[:, at], prod[head, at]], axis=0)
        wins = [own_part[(n - 1) * span:(n + 1) * span] for n in range(1, blocks)]
        return jnp.concatenate([first] + wins, axis=1)

    def conv(c, mats, wins):
        stack = mats[pl.ds(pl.multiple_of(c * per_chunk, per_chunk), per_chunk)]
        y = jnp.dot(stack.reshape(per_chunk * span, 2 * span), wins,
                    preferred_element_type=F32).astype(BF16)
        out = y[:span]
        for j in range(1, per_chunk):
            out = jnp.where(member == j, y[j * span:(j + 1) * span], out)
        return jnp.concatenate(
            [out[:, n * WIDE:(n + 1) * WIDE] for n in range(blocks)], axis=0)

    chunks = PART // WIDE

    def correlate(c):
        at = pl.ds(pl.multiple_of(c * WIDE, WIDE), WIDE)
        wins = g_windows(at).T
        left = jnp.concatenate(
            [prod[n * span:(n + 1) * span, at] for n in range(blocks)], axis=1)
        mine = jnp.concatenate(
            [jnp.where(member == j, left, jnp.zeros_like(left)) for j in range(per_chunk)], axis=0)
        every = jnp.dot(mine, wins, preferred_element_type=F32)
        for j in range(per_chunk):
            both = every[j * span:(j + 1) * span]
            turn = jnp.where(upper, both[:, :span], both[:, span:])
            half = span // 2
            while half >= 8:
                turn = turn[:half] + pltpu.roll(turn[half:], span - half, 1)
                half //= 2
            folded[pl.ds(pl.multiple_of((c * per_chunk + j) * 8, 8), 8), :] = turn

    @pl.loop(0, parts)
    def _(i):
        @pl.when(me < n_ctx - 1)
        def _():
            g_copy(i).wait_recv()

        for c in range(chunks):
            correlate(i * chunks + c)

    total = folded[pl.ds(0, groups, stride=8), :]
    for r in range(1, 8):
        total = total + pltpu.roll(folded[pl.ds(r, groups, stride=8), :], span - r, 1)
    partial[...] = total.reshape(partial.shape)

    def rs_copy(to, sender):
        return pltpu.make_async_remote_copy(
            src_ref=partial.at[to], dst_ref=arrived.at[sender],
            send_sem=rs_send.at[to], recv_sem=rs_recv.at[sender],
            device_id=(to, slab), device_id_type=MESH)

    def ag_copy(to, sender):
        return pltpu.make_async_remote_copy(
            src_ref=reduced, dst_ref=gathered.at[sender],
            send_sem=ag_send.at[to], recv_sem=ag_recv.at[sender],
            device_id=(to, slab), device_id_type=MESH)

    def sq_copy(to, sender):
        return pltpu.make_async_remote_copy(
            src_ref=own_sq, dst_ref=all_sq.at[sender],
            send_sem=sq_send.at[to], recv_sem=sq_recv.at[sender],
            device_id=(me, to), device_id_type=MESH)

    @pl.loop(1, n_ctx)
    def _(i):
        rs_copy(ctx_peer(i), me).start()

    arrived[me] = partial[me]

    def both_convs(c):
        at = pl.ds(pl.multiple_of(c * WIDE, WIDE), WIDE)
        back = conv(c, toep, g_windows(at))
        ahead = conv(c, toep_f, p_windows(at))
        gk_ref[:, at] = times(back, v_ref[:, at])
        gv_ref[:, at] = times(back, k_ref[:, at])
        mix_ref[:, at] = times(ahead, q_ref[:, at])
        gq_ref[:, at] = times(ahead, g_ref[:, at])

    def gather_rows():
        @pl.loop(1, n_ctx)
        def _(i):
            rs_copy(me, ctx_peer(i)).wait_recv()

        reduced[...] = jnp.sum(arrived[...], axis=0)

        @pl.loop(1, n_ctx)
        def _(i):
            ag_copy(ctx_peer(i), me).start()

        gathered[me] = reduced[...]

    def share_squares():
        @pl.loop(1, n_ctx)
        def _(i):
            ag_copy(me, ctx_peer(i)).wait_recv()

        raw = gathered[...].reshape(groups, span)
        squares = jnp.sum(jnp.sum(raw * raw, axis=0, keepdims=True), axis=1, keepdims=True)
        own_sq[...] = jnp.broadcast_to(squares, own_sq.shape)

        @pl.loop(1, n_mp)
        def _(i):
            sq_copy(mp_peer(i), slab).start()

        all_sq[slab] = own_sq[...]

    @pl.loop(0, parts)
    def _(i):
        pl.when(i == parts * 3 // 8)(gather_rows)
        pl.when(i == parts * 6 // 8)(share_squares)

        @pl.when(me > 0)
        def _():
            p_copy(i).wait_recv()

        for c in range(chunks):
            both_convs(i * chunks + c)

    @pl.loop(1, n_mp)
    def _(i):
        sq_copy(slab, mp_peer(i)).wait_recv()

    raw = gathered[...].reshape(groups, span)
    square_sum = jnp.sum(all_sq[...], axis=0)[0:1, :]
    grad_rms = jnp.sqrt(square_sum / (groups * n_mp * span) + 1e-06)
    gf_ref[...] = raw * jnp.minimum(1.0, 1.0 / grad_rms)

    @pl.loop(0, parts)
    def _(i):
        @pl.when(me > 0)
        def _():
            g_copy(i).wait_send()

        @pl.when(me < n_ctx - 1)
        def _():
            p_copy(i).wait_send()

    @pl.loop(1, n_ctx)
    def _(i):
        rs_copy(ctx_peer(i), me).wait_send()
        ag_copy(ctx_peer(i), me).wait_send()

    @pl.loop(1, n_mp)
    def _(i):
        sq_copy(mp_peer(i), slab).wait_send()


def unload(a, b, c, d, e, ao, bo, co, do, eo, sems):
    copies = [pltpu.make_async_copy(x, y, sems.at[i]) for i, (x, y) in enumerate(
        zip((a, b, c, d, e), (ao, bo, co, do, eo)))]
    for copy in copies:
        copy.start()
    for copy in copies:
        copy.wait()


def shards(queries, key_feats, value_feats, filters, grad_out):
    n_ctx, n_mp = lax.axis_size("ctx"), lax.axis_size("mp")
    tokens, channels = queries.shape
    groups, span = filters.shape
    own = groups // n_ctx
    vmem = pl.BlockSpec(memory_space=pltpu.VMEM)
    dma = pltpu.SemaphoreType.DMA
    like = pltpu.VMEM((tokens, channels), BF16)
    anywhere = pl.BlockSpec(memory_space=pl.ANY)
    parts = channels // PART
    results = pl.pallas_call(
        functools.partial(kernel, n_ctx, n_mp),
        out_shape=(like, like, like, like, pltpu.VMEM((groups, span), F32)),
        in_specs=[anywhere] * 3 + [vmem, anywhere],
        out_specs=[vmem] * 5,
        scratch_shapes=[
            pltpu.VMEM((tokens, channels), BF16),
            pltpu.VMEM((tokens, channels), BF16),
            pltpu.VMEM((tokens, channels), BF16),
            pltpu.VMEM((tokens, channels), BF16),
            pltpu.VMEM((tokens, channels), BF16),
            pltpu.VMEM((tokens, channels), BF16),
            pltpu.VMEM((span, channels), BF16),
            pltpu.VMEM((span, channels), BF16),
            pltpu.VMEM((groups, span), F32),
            pltpu.VMEM((groups, span), F32),
            pltpu.VMEM((groups, span, 2 * span), BF16),
            pltpu.VMEM((groups, span, 2 * span), BF16),
            pltpu.VMEM((8 * groups, span), F32),
            pltpu.VMEM((n_ctx, own, span), F32),
            pltpu.VMEM((n_ctx, own, span), F32),
            pltpu.VMEM((own, span), F32),
            pltpu.VMEM((n_ctx, own, span), F32),
            pltpu.VMEM((8, span), F32),
            pltpu.VMEM((n_mp, 8, span), F32),
            dma((parts,)), dma((parts,)), dma((parts,)), dma((parts,)),
            dma((n_ctx,)), dma((n_ctx,)), dma((n_ctx,)), dma((n_ctx,)),
            dma((n_mp,)), dma((n_mp,)), dma((8,)),
        ],
        compiler_params=pltpu.CompilerParams(
            collective_id=0, has_side_effects=True, vmem_limit_bytes=56 * 2**20),
    )(queries, key_feats, value_feats, filters, grad_out)
    return pl.pallas_call(
        unload,
        out_shape=tuple(jax.ShapeDtypeStruct(x.shape, x.dtype) for x in results),
        in_specs=[anywhere] * 5,
        out_specs=[anywhere] * 5,
        scratch_shapes=[dma((5,))],
        compiler_params=pltpu.CompilerParams(vmem_limit_bytes=8 * 2**20),
    )(*results)


def solution(mesh):
    placed = (P("ctx", "mp"), P("ctx", "mp"), P("ctx", "mp"), P("mp", None), P("ctx", "mp"))
    return jax.shard_map(
        shards,
        mesh=mesh,
        in_specs=placed,
        out_specs=(P("ctx", "mp"), P("ctx", "mp"), P("ctx", "mp"), P("ctx", "mp"), P("mp", None)),
        check_vma=False,
    )
```

```python
import functools

import jax
import jax.numpy as jnp
from jax import lax
from jax.experimental import pallas as pl
from jax.experimental.pallas import tpu as pltpu
from jax.sharding import PartitionSpec as P

G = 16
MESH = pl.DeviceIdType.MESH
F32 = jnp.float32
BF16 = jnp.bfloat16
WIDE = 128
PART = 256


def times(a, b):
    return (a.astype(F32) * b.astype(F32)).astype(BF16)


def kernel(n_ctx, n_mp, q_hbm, k_hbm, v_hbm, f_ref, g_hbm,
           mix_ref, gq_ref, gk_ref, gv_ref, gf_ref,
           q_ref, k_ref, v_ref, g_ref, prod, gmix, phalo, ghalo, taps, flipped, toep, toep_f, folded,
           partial, arrived, reduced, gathered, own_sq, all_sq,
           p_send, p_recv, g_send, g_recv,
           rs_send, rs_recv, ag_send, ag_recv, sq_send, sq_recv, load):
    tokens, channels = q_ref.shape
    groups, span = f_ref.shape
    blocks = tokens // span
    own = groups // n_ctx
    parts = channels // PART
    me = lax.axis_index("ctx")
    slab = lax.axis_index("mp")
    per_chunk = WIDE // G

    def ctx_peer(i):
        return lax.rem(me + i, n_ctx)

    def mp_peer(i):
        return lax.rem(slab + i, n_mp)

    barrier = pltpu.get_barrier_semaphore()

    @pl.loop(1, n_ctx)
    def _(i):
        pl.semaphore_signal(barrier, inc=1, device_id=(ctx_peer(i), slab), device_id_type=MESH)

    @pl.loop(1, n_mp)
    def _(i):
        pl.semaphore_signal(barrier, inc=1, device_id=(me, mp_peer(i)), device_id_type=MESH)

    head, tail = slice(0, span), slice(tokens - span, tokens)
    rest_g, rest_p = slice(span, tokens), slice(0, tokens - span)

    def loads(pairs, first):
        return [pltpu.make_async_copy(a.at[rows, :], b.at[rows, :], load.at[first + i])
                for i, (a, b, rows) in enumerate(pairs)]

    edges = loads([(g_hbm, g_ref, head), (q_hbm, q_ref, head)], 0)
    others = loads([(k_hbm, k_ref, tail), (v_hbm, v_ref, tail),
                    (g_hbm, g_ref, rest_g), (q_hbm, q_ref, rest_g),
                    (k_hbm, k_ref, rest_p), (v_hbm, v_ref, rest_p)], 2)
    for copy in edges + others:
        copy.start()
    for copy in edges:
        copy.wait()
    pl.semaphore_wait(barrier, n_ctx + n_mp - 2)

    def g_copy(i):
        cols = pl.ds(pl.multiple_of(i * PART, PART), PART)
        return pltpu.make_async_remote_copy(
            src_ref=gmix.at[head, cols], dst_ref=ghalo.at[:, cols],
            send_sem=g_send.at[i], recv_sem=g_recv.at[i],
            device_id=(lax.rem(me + n_ctx - 1, n_ctx), slab), device_id_type=MESH)

    def p_copy(i):
        cols = pl.ds(pl.multiple_of(i * PART, PART), PART)
        return pltpu.make_async_remote_copy(
            src_ref=prod.at[tail, cols], dst_ref=phalo.at[:, cols],
            send_sem=p_send.at[i], recv_sem=p_recv.at[i],
            device_id=(lax.rem(me + 1, n_ctx), slab), device_id_type=MESH)

    @pl.loop(0, parts)
    def _(i):
        cols = pl.ds(pl.multiple_of(i * PART, PART), PART)
        gmix[head, cols] = times(g_ref[head, cols], q_ref[head, cols])

        @pl.when(me > 0)
        def _():
            g_copy(i).start()

    @pl.when(me == 0)
    def _():
        phalo[...] = jnp.zeros_like(phalo)

    @pl.when(me == n_ctx - 1)
    def _():
        ghalo[...] = jnp.zeros_like(ghalo)

    for copy in others:
        copy.wait()

    @pl.loop(0, parts)
    def _(i):
        cols = pl.ds(pl.multiple_of(i * PART, PART), PART)
        gmix[rest_g, cols] = times(g_ref[rest_g, cols], q_ref[rest_g, cols])
        prod[:, cols] = times(k_ref[:, cols], v_ref[:, cols])

    taps[...] = f_ref[...].astype(F32)

    col = lax.broadcasted_iota(jnp.int32, (span, span), 1)
    row = lax.broadcasted_iota(jnp.int32, (span, span), 0)
    upper = col >= row

    flip = jnp.where(lax.rem(row + col, span) == 0, 1.0, 0.0).astype(BF16)
    flipped[...] = jnp.dot(f_ref[...], flip, preferred_element_type=F32)

    def spread(i, lines, out, mask):
        line = jnp.broadcast_to(lines[pl.ds(i, 1), :], (span, span))
        turned = pltpu.roll(line, 0, 1, stride=1, stride_axis=0)
        zero = jnp.zeros_like(turned)
        out[i, :, 0:span] = jnp.where(mask, turned, zero).astype(BF16)
        out[i, :, span:] = jnp.where(mask, zero, turned).astype(BF16)

    def build(c):
        for j in range(per_chunk):
            spread(c * per_chunk + j, taps, toep, upper)
            spread(c * per_chunk + j, flipped, toep_f, col > row)

    lane = lax.broadcasted_iota(jnp.int32, (1, blocks * WIDE), 1)
    member = lax.rem(lane, WIDE) // G

    def g_windows(at):
        own_part = gmix[:, at]
        last = jnp.concatenate([gmix[tail, at], ghalo[:, at]], axis=0)
        wins = [own_part[n * span:(n + 2) * span] for n in range(blocks - 1)]
        return jnp.concatenate(wins + [last], axis=1)

    def p_windows(at):
        own_part = prod[:, at]
        first = jnp.concatenate([phalo[:, at], prod[head, at]], axis=0)
        wins = [own_part[(n - 1) * span:(n + 1) * span] for n in range(1, blocks)]
        return jnp.concatenate([first] + wins, axis=1)

    def conv(c, mats, wins):
        stack = mats[pl.ds(pl.multiple_of(c * per_chunk, per_chunk), per_chunk)]
        y = jnp.dot(stack.reshape(per_chunk * span, 2 * span), wins,
                    preferred_element_type=F32).astype(BF16)
        out = y[:span]
        for j in range(1, per_chunk):
            out = jnp.where(member == j, y[j * span:(j + 1) * span], out)
        return jnp.concatenate(
            [out[:, n * WIDE:(n + 1) * WIDE] for n in range(blocks)], axis=0)

    chunks = PART // WIDE

    def correlate(c):
        at = pl.ds(pl.multiple_of(c * WIDE, WIDE), WIDE)
        wins = g_windows(at)
        left = jnp.concatenate(
            [prod[n * span:(n + 1) * span, at] for n in range(blocks)], axis=1)
        mine = jnp.concatenate(
            [jnp.where(member == j, left, jnp.zeros_like(left)) for j in range(per_chunk)], axis=0)
        every = lax.dot_general(mine, wins, (((1,), (1,)), ((), ())),
                                preferred_element_type=F32)
        for j in range(per_chunk):
            both = every[j * span:(j + 1) * span]
            turn = jnp.where(upper, both[:, :span], both[:, span:])
            half = span // 2
            while half >= 8:
                turn = turn[:half] + pltpu.roll(turn[half:], span - half, 1)
                half //= 2
            folded[pl.ds(pl.multiple_of((c * per_chunk + j) * 8, 8), 8), :] = turn

    @pl.loop(0, parts)
    def _(i):
        @pl.when(me < n_ctx - 1)
        def _():
            g_copy(i).wait_recv()

        @pl.when(me < n_ctx - 1)
        def _():
            p_copy(i).start()

        for c in range(chunks):
            build(i * chunks + c)
            correlate(i * chunks + c)

    total = folded[pl.ds(0, groups, stride=8), :]
    for r in range(1, 8):
        total = total + pltpu.roll(folded[pl.ds(r, groups, stride=8), :], span - r, 1)
    partial[...] = total.reshape(partial.shape)

    def rs_copy(to, sender):
        return pltpu.make_async_remote_copy(
            src_ref=partial.at[to], dst_ref=arrived.at[sender],
            send_sem=rs_send.at[to], recv_sem=rs_recv.at[sender],
            device_id=(to, slab), device_id_type=MESH)

    def ag_copy(to, sender):
        return pltpu.make_async_remote_copy(
            src_ref=reduced, dst_ref=gathered.at[sender],
            send_sem=ag_send.at[to], recv_sem=ag_recv.at[sender],
            device_id=(to, slab), device_id_type=MESH)

    def sq_copy(to, sender):
        return pltpu.make_async_remote_copy(
            src_ref=own_sq, dst_ref=all_sq.at[sender],
            send_sem=sq_send.at[to], recv_sem=sq_recv.at[sender],
            device_id=(me, to), device_id_type=MESH)

    @pl.loop(1, n_ctx)
    def _(i):
        rs_copy(ctx_peer(i), me).start()

    arrived[me] = partial[me]

    def both_convs(c):
        at = pl.ds(pl.multiple_of(c * WIDE, WIDE), WIDE)
        back = conv(c, toep, g_windows(at))
        ahead = conv(c, toep_f, p_windows(at))
        gk_ref[:, at] = times(back, v_ref[:, at])
        gv_ref[:, at] = times(back, k_ref[:, at])
        mix_ref[:, at] = times(ahead, q_ref[:, at])
        gq_ref[:, at] = times(ahead, g_ref[:, at])

    def gather_rows():
        @pl.loop(1, n_ctx)
        def _(i):
            rs_copy(me, ctx_peer(i)).wait_recv()

        reduced[...] = jnp.sum(arrived[...], axis=0)

        @pl.loop(1, n_ctx)
        def _(i):
            ag_copy(ctx_peer(i), me).start()

        gathered[me] = reduced[...]

    def share_squares():
        @pl.loop(1, n_ctx)
        def _(i):
            ag_copy(me, ctx_peer(i)).wait_recv()

        raw = gathered[...].reshape(groups, span)
        squares = jnp.sum(jnp.sum(raw * raw, axis=0, keepdims=True), axis=1, keepdims=True)
        own_sq[...] = jnp.broadcast_to(squares, own_sq.shape)

        @pl.loop(1, n_mp)
        def _(i):
            sq_copy(mp_peer(i), slab).start()

        all_sq[slab] = own_sq[...]

    @pl.loop(0, parts)
    def _(i):
        pl.when(i == parts * 3 // 8)(gather_rows)
        pl.when(i == parts * 6 // 8)(share_squares)

        @pl.when(me > 0)
        def _():
            p_copy(i).wait_recv()

        for c in range(chunks):
            both_convs(i * chunks + c)

    @pl.loop(1, n_mp)
    def _(i):
        sq_copy(slab, mp_peer(i)).wait_recv()

    raw = gathered[...].reshape(groups, span)
    square_sum = jnp.sum(all_sq[...], axis=0)[0:1, :]
    grad_rms = jnp.sqrt(square_sum / (groups * n_mp * span) + 1e-06)
    gf_ref[...] = raw * jnp.minimum(1.0, 1.0 / grad_rms)

    @pl.loop(0, parts)
    def _(i):
        @pl.when(me > 0)
        def _():
            g_copy(i).wait_send()

        @pl.when(me < n_ctx - 1)
        def _():
            p_copy(i).wait_send()

    @pl.loop(1, n_ctx)
    def _(i):
        rs_copy(ctx_peer(i), me).wait_send()
        ag_copy(ctx_peer(i), me).wait_send()

    @pl.loop(1, n_mp)
    def _(i):
        sq_copy(mp_peer(i), slab).wait_send()


def unload(a, b, c, d, e, ao, bo, co, do, eo, sems):
    copies = [pltpu.make_async_copy(x, y, sems.at[i]) for i, (x, y) in enumerate(
        zip((a, b, c, d, e), (ao, bo, co, do, eo)))]
    for copy in copies:
        copy.start()
    for copy in copies:
        copy.wait()


def shards(queries, key_feats, value_feats, filters, grad_out):
    n_ctx, n_mp = lax.axis_size("ctx"), lax.axis_size("mp")
    tokens, channels = queries.shape
    groups, span = filters.shape
    own = groups // n_ctx
    vmem = pl.BlockSpec(memory_space=pltpu.VMEM)
    dma = pltpu.SemaphoreType.DMA
    like = pltpu.VMEM((tokens, channels), BF16)
    anywhere = pl.BlockSpec(memory_space=pl.ANY)
    parts = channels // PART
    results = pl.pallas_call(
        functools.partial(kernel, n_ctx, n_mp),
        out_shape=(like, like, like, like, pltpu.VMEM((groups, span), F32)),
        in_specs=[anywhere] * 3 + [vmem, anywhere],
        out_specs=[vmem] * 5,
        scratch_shapes=[
            pltpu.VMEM((tokens, channels), BF16),
            pltpu.VMEM((tokens, channels), BF16),
            pltpu.VMEM((tokens, channels), BF16),
            pltpu.VMEM((tokens, channels), BF16),
            pltpu.VMEM((tokens, channels), BF16),
            pltpu.VMEM((tokens, channels), BF16),
            pltpu.VMEM((span, channels), BF16),
            pltpu.VMEM((span, channels), BF16),
            pltpu.VMEM((groups, span), F32),
            pltpu.VMEM((groups, span), F32),
            pltpu.VMEM((groups, span, 2 * span), BF16),
            pltpu.VMEM((groups, span, 2 * span), BF16),
            pltpu.VMEM((8 * groups, span), F32),
            pltpu.VMEM((n_ctx, own, span), F32),
            pltpu.VMEM((n_ctx, own, span), F32),
            pltpu.VMEM((own, span), F32),
            pltpu.VMEM((n_ctx, own, span), F32),
            pltpu.VMEM((8, span), F32),
            pltpu.VMEM((n_mp, 8, span), F32),
            dma((parts,)), dma((parts,)), dma((parts,)), dma((parts,)),
            dma((n_ctx,)), dma((n_ctx,)), dma((n_ctx,)), dma((n_ctx,)),
            dma((n_mp,)), dma((n_mp,)), dma((8,)),
        ],
        compiler_params=pltpu.CompilerParams(
            collective_id=0, has_side_effects=True, vmem_limit_bytes=56 * 2**20),
    )(queries, key_feats, value_feats, filters, grad_out)
    return pl.pallas_call(
        unload,
        out_shape=tuple(jax.ShapeDtypeStruct(x.shape, x.dtype) for x in results),
        in_specs=[anywhere] * 5,
        out_specs=[anywhere] * 5,
        scratch_shapes=[dma((5,))],
        compiler_params=pltpu.CompilerParams(vmem_limit_bytes=8 * 2**20),
    )(*results)


def solution(mesh):
    placed = (P("ctx", "mp"), P("ctx", "mp"), P("ctx", "mp"), P("mp", None), P("ctx", "mp"))
    return jax.shard_map(
        shards,
        mesh=mesh,
        in_specs=placed,
        out_specs=(P("ctx", "mp"), P("ctx", "mp"), P("ctx", "mp"), P("ctx", "mp"), P("mp", None)),
        check_vma=False,
    )
```

```python
import functools

import jax
import jax.numpy as jnp
from jax import lax
from jax.experimental import pallas as pl
from jax.experimental.pallas import tpu as pltpu
from jax.sharding import PartitionSpec as P

G = 16
MESH = pl.DeviceIdType.MESH
F32 = jnp.float32
BF16 = jnp.bfloat16
WIDE = 128
PART = 512


def times(a, b):
    return (a.astype(F32) * b.astype(F32)).astype(BF16)


def kernel(n_ctx, n_mp, q_hbm, k_hbm, v_hbm, f_ref, g_hbm,
           mix_ref, gq_ref, gk_ref, gv_ref, gf_ref,
           q_ref, k_ref, v_ref, g_ref, prod, gmix, phalo, ghalo, taps, flipped, toep, toep_f, folded,
           partial, arrived, reduced, gathered, own_sq, all_sq,
           p_send, p_recv, g_send, g_recv,
           rs_send, rs_recv, ag_send, ag_recv, sq_send, sq_recv, load):
    tokens, channels = q_ref.shape
    groups, span = f_ref.shape
    blocks = tokens // span
    own = groups // n_ctx
    parts = channels // PART
    me = lax.axis_index("ctx")
    slab = lax.axis_index("mp")
    per_chunk = WIDE // G

    def ctx_peer(i):
        return lax.rem(me + i, n_ctx)

    def mp_peer(i):
        return lax.rem(slab + i, n_mp)

    barrier = pltpu.get_barrier_semaphore()

    @pl.loop(1, n_ctx)
    def _(i):
        pl.semaphore_signal(barrier, inc=1, device_id=(ctx_peer(i), slab), device_id_type=MESH)

    @pl.loop(1, n_mp)
    def _(i):
        pl.semaphore_signal(barrier, inc=1, device_id=(me, mp_peer(i)), device_id_type=MESH)

    head, tail = slice(0, span), slice(tokens - span, tokens)
    rest_g, rest_p = slice(span, tokens), slice(0, tokens - span)

    def loads(pairs, first):
        return [pltpu.make_async_copy(a.at[rows, :], b.at[rows, :], load.at[first + i])
                for i, (a, b, rows) in enumerate(pairs)]

    edges = loads([(g_hbm, g_ref, head), (q_hbm, q_ref, head)], 0)
    others = loads([(k_hbm, k_ref, tail), (v_hbm, v_ref, tail),
                    (g_hbm, g_ref, rest_g), (q_hbm, q_ref, rest_g),
                    (k_hbm, k_ref, rest_p), (v_hbm, v_ref, rest_p)], 2)
    for copy in edges + others:
        copy.start()
    for copy in edges:
        copy.wait()
    pl.semaphore_wait(barrier, n_ctx + n_mp - 2)

    def g_copy(i):
        cols = pl.ds(pl.multiple_of(i * PART, PART), PART)
        return pltpu.make_async_remote_copy(
            src_ref=gmix.at[head, cols], dst_ref=ghalo.at[:, cols],
            send_sem=g_send.at[i], recv_sem=g_recv.at[i],
            device_id=(lax.rem(me + n_ctx - 1, n_ctx), slab), device_id_type=MESH)

    def p_copy(i):
        cols = pl.ds(pl.multiple_of(i * PART, PART), PART)
        return pltpu.make_async_remote_copy(
            src_ref=prod.at[tail, cols], dst_ref=phalo.at[:, cols],
            send_sem=p_send.at[i], recv_sem=p_recv.at[i],
            device_id=(lax.rem(me + 1, n_ctx), slab), device_id_type=MESH)

    @pl.loop(0, parts)
    def _(i):
        cols = pl.ds(pl.multiple_of(i * PART, PART), PART)
        gmix[head, cols] = times(g_ref[head, cols], q_ref[head, cols])

        @pl.when(me > 0)
        def _():
            g_copy(i).start()

    @pl.when(me == 0)
    def _():
        phalo[...] = jnp.zeros_like(phalo)

    @pl.when(me == n_ctx - 1)
    def _():
        ghalo[...] = jnp.zeros_like(ghalo)

    for copy in others:
        copy.wait()

    @pl.loop(0, parts)
    def _(i):
        cols = pl.ds(pl.multiple_of(i * PART, PART), PART)
        gmix[rest_g, cols] = times(g_ref[rest_g, cols], q_ref[rest_g, cols])
        prod[:, cols] = times(k_ref[:, cols], v_ref[:, cols])

    taps[...] = f_ref[...].astype(F32)

    col = lax.broadcasted_iota(jnp.int32, (span, span), 1)
    row = lax.broadcasted_iota(jnp.int32, (span, span), 0)
    upper = col >= row

    flip = jnp.where(lax.rem(row + col, span) == 0, 1.0, 0.0).astype(BF16)
    flipped[...] = jnp.dot(f_ref[...], flip, preferred_element_type=F32)

    def spread(i, lines, out, mask):
        line = jnp.broadcast_to(lines[pl.ds(i, 1), :], (span, span))
        turned = pltpu.roll(line, 0, 1, stride=1, stride_axis=0)
        zero = jnp.zeros_like(turned)
        out[i, :, 0:span] = jnp.where(mask, turned, zero).astype(BF16)
        out[i, :, span:] = jnp.where(mask, zero, turned).astype(BF16)

    def build(c):
        for j in range(per_chunk):
            spread(c * per_chunk + j, taps, toep, upper)
            spread(c * per_chunk + j, flipped, toep_f, col > row)

    lane = lax.broadcasted_iota(jnp.int32, (1, blocks * WIDE), 1)
    member = lax.rem(lane, WIDE) // G

    def g_windows(at):
        own_part = gmix[:, at]
        last = jnp.concatenate([gmix[tail, at], ghalo[:, at]], axis=0)
        wins = [own_part[n * span:(n + 2) * span] for n in range(blocks - 1)]
        return jnp.concatenate(wins + [last], axis=1)

    def p_windows(at):
        own_part = prod[:, at]
        first = jnp.concatenate([phalo[:, at], prod[head, at]], axis=0)
        wins = [own_part[(n - 1) * span:(n + 1) * span] for n in range(1, blocks)]
        return jnp.concatenate([first] + wins, axis=1)

    def conv(c, mats, wins):
        stack = mats[pl.ds(pl.multiple_of(c * per_chunk, per_chunk), per_chunk)]
        y = jnp.dot(stack.reshape(per_chunk * span, 2 * span), wins,
                    preferred_element_type=F32).astype(BF16)
        out = y[:span]
        for j in range(1, per_chunk):
            out = jnp.where(member == j, y[j * span:(j + 1) * span], out)
        return jnp.concatenate(
            [out[:, n * WIDE:(n + 1) * WIDE] for n in range(blocks)], axis=0)

    chunks = PART // WIDE

    def correlate(c):
        at = pl.ds(pl.multiple_of(c * WIDE, WIDE), WIDE)
        wins = g_windows(at)
        left = jnp.concatenate(
            [prod[n * span:(n + 1) * span, at] for n in range(blocks)], axis=1)
        mine = jnp.concatenate(
            [jnp.where(member == j, left, jnp.zeros_like(left)) for j in range(per_chunk)], axis=0)
        every = lax.dot_general(mine, wins, (((1,), (1,)), ((), ())),
                                preferred_element_type=F32)
        for j in range(per_chunk):
            both = every[j * span:(j + 1) * span]
            turn = jnp.where(upper, both[:, :span], both[:, span:])
            half = span // 2
            while half >= 8:
                turn = turn[:half] + pltpu.roll(turn[half:], span - half, 1)
                half //= 2
            folded[pl.ds(pl.multiple_of((c * per_chunk + j) * 8, 8), 8), :] = turn

    @pl.loop(0, parts)
    def _(i):
        @pl.when(me < n_ctx - 1)
        def _():
            g_copy(i).wait_recv()

        @pl.when(me < n_ctx - 1)
        def _():
            p_copy(i).start()

        for c in range(chunks):
            build(i * chunks + c)
            correlate(i * chunks + c)

    total = folded[pl.ds(0, groups, stride=8), :]
    for r in range(1, 8):
        total = total + pltpu.roll(folded[pl.ds(r, groups, stride=8), :], span - r, 1)
    partial[...] = total.reshape(partial.shape)

    def rs_copy(to, sender):
        return pltpu.make_async_remote_copy(
            src_ref=partial.at[to], dst_ref=arrived.at[sender],
            send_sem=rs_send.at[to], recv_sem=rs_recv.at[sender],
            device_id=(to, slab), device_id_type=MESH)

    def ag_copy(to, sender):
        return pltpu.make_async_remote_copy(
            src_ref=reduced, dst_ref=gathered.at[sender],
            send_sem=ag_send.at[to], recv_sem=ag_recv.at[sender],
            device_id=(to, slab), device_id_type=MESH)

    def sq_copy(to, sender):
        return pltpu.make_async_remote_copy(
            src_ref=own_sq, dst_ref=all_sq.at[sender],
            send_sem=sq_send.at[to], recv_sem=sq_recv.at[sender],
            device_id=(me, to), device_id_type=MESH)

    @pl.loop(1, n_ctx)
    def _(i):
        rs_copy(ctx_peer(i), me).start()

    arrived[me] = partial[me]

    def both_convs(c):
        at = pl.ds(pl.multiple_of(c * WIDE, WIDE), WIDE)
        back = conv(c, toep, g_windows(at))
        ahead = conv(c, toep_f, p_windows(at))
        gk_ref[:, at] = times(back, v_ref[:, at])
        gv_ref[:, at] = times(back, k_ref[:, at])
        mix_ref[:, at] = times(ahead, q_ref[:, at])
        gq_ref[:, at] = times(ahead, g_ref[:, at])

    def gather_rows():
        @pl.loop(1, n_ctx)
        def _(i):
            rs_copy(me, ctx_peer(i)).wait_recv()

        reduced[...] = jnp.sum(arrived[...], axis=0)

        @pl.loop(1, n_ctx)
        def _(i):
            ag_copy(ctx_peer(i), me).start()

        gathered[me] = reduced[...]

    def share_squares():
        @pl.loop(1, n_ctx)
        def _(i):
            ag_copy(me, ctx_peer(i)).wait_recv()

        raw = gathered[...].reshape(groups, span)
        squares = jnp.sum(jnp.sum(raw * raw, axis=0, keepdims=True), axis=1, keepdims=True)
        own_sq[...] = jnp.broadcast_to(squares, own_sq.shape)

        @pl.loop(1, n_mp)
        def _(i):
            sq_copy(mp_peer(i), slab).start()

        all_sq[slab] = own_sq[...]

    @pl.loop(0, parts)
    def _(i):
        pl.when(i == parts * 3 // 8)(gather_rows)
        pl.when(i == parts * 6 // 8)(share_squares)

        @pl.when(me > 0)
        def _():
            p_copy(i).wait_recv()

        for c in range(chunks):
            both_convs(i * chunks + c)

    @pl.loop(1, n_mp)
    def _(i):
        sq_copy(slab, mp_peer(i)).wait_recv()

    raw = gathered[...].reshape(groups, span)
    square_sum = jnp.sum(all_sq[...], axis=0)[0:1, :]
    grad_rms = jnp.sqrt(square_sum / (groups * n_mp * span) + 1e-06)
    gf_ref[...] = raw * jnp.minimum(1.0, 1.0 / grad_rms)

    @pl.loop(0, parts)
    def _(i):
        @pl.when(me > 0)
        def _():
            g_copy(i).wait_send()

        @pl.when(me < n_ctx - 1)
        def _():
            p_copy(i).wait_send()

    @pl.loop(1, n_ctx)
    def _(i):
        rs_copy(ctx_peer(i), me).wait_send()
        ag_copy(ctx_peer(i), me).wait_send()

    @pl.loop(1, n_mp)
    def _(i):
        sq_copy(mp_peer(i), slab).wait_send()


def unload(a, b, c, d, e, ao, bo, co, do, eo, sems):
    copies = [pltpu.make_async_copy(x, y, sems.at[i]) for i, (x, y) in enumerate(
        zip((a, b, c, d, e), (ao, bo, co, do, eo)))]
    for copy in copies:
        copy.start()
    for copy in copies:
        copy.wait()


def shards(queries, key_feats, value_feats, filters, grad_out):
    n_ctx, n_mp = lax.axis_size("ctx"), lax.axis_size("mp")
    tokens, channels = queries.shape
    groups, span = filters.shape
    own = groups // n_ctx
    vmem = pl.BlockSpec(memory_space=pltpu.VMEM)
    dma = pltpu.SemaphoreType.DMA
    like = pltpu.VMEM((tokens, channels), BF16)
    anywhere = pl.BlockSpec(memory_space=pl.ANY)
    parts = channels // PART
    results = pl.pallas_call(
        functools.partial(kernel, n_ctx, n_mp),
        out_shape=(like, like, like, like, pltpu.VMEM((groups, span), F32)),
        in_specs=[anywhere] * 3 + [vmem, anywhere],
        out_specs=[vmem] * 5,
        scratch_shapes=[
            pltpu.VMEM((tokens, channels), BF16),
            pltpu.VMEM((tokens, channels), BF16),
            pltpu.VMEM((tokens, channels), BF16),
            pltpu.VMEM((tokens, channels), BF16),
            pltpu.VMEM((tokens, channels), BF16),
            pltpu.VMEM((tokens, channels), BF16),
            pltpu.VMEM((span, channels), BF16),
            pltpu.VMEM((span, channels), BF16),
            pltpu.VMEM((groups, span), F32),
            pltpu.VMEM((groups, span), F32),
            pltpu.VMEM((groups, span, 2 * span), BF16),
            pltpu.VMEM((groups, span, 2 * span), BF16),
            pltpu.VMEM((8 * groups, span), F32),
            pltpu.VMEM((n_ctx, own, span), F32),
            pltpu.VMEM((n_ctx, own, span), F32),
            pltpu.VMEM((own, span), F32),
            pltpu.VMEM((n_ctx, own, span), F32),
            pltpu.VMEM((8, span), F32),
            pltpu.VMEM((n_mp, 8, span), F32),
            dma((parts,)), dma((parts,)), dma((parts,)), dma((parts,)),
            dma((n_ctx,)), dma((n_ctx,)), dma((n_ctx,)), dma((n_ctx,)),
            dma((n_mp,)), dma((n_mp,)), dma((8,)),
        ],
        compiler_params=pltpu.CompilerParams(
            collective_id=0, has_side_effects=True, vmem_limit_bytes=56 * 2**20),
    )(queries, key_feats, value_feats, filters, grad_out)
    return pl.pallas_call(
        unload,
        out_shape=tuple(jax.ShapeDtypeStruct(x.shape, x.dtype) for x in results),
        in_specs=[anywhere] * 5,
        out_specs=[anywhere] * 5,
        scratch_shapes=[dma((5,))],
        compiler_params=pltpu.CompilerParams(vmem_limit_bytes=8 * 2**20),
    )(*results)


def solution(mesh):
    placed = (P("ctx", "mp"), P("ctx", "mp"), P("ctx", "mp"), P("mp", None), P("ctx", "mp"))
    return jax.shard_map(
        shards,
        mesh=mesh,
        in_specs=placed,
        out_specs=(P("ctx", "mp"), P("ctx", "mp"), P("ctx", "mp"), P("ctx", "mp"), P("mp", None)),
        check_vma=False,
    )
```
